512 devices in a mesh: tm: 128 (over z_lo, x, y), rows: 4 (over z_hi, core).
Axes of the slice: x: 4, y: 8, z: 8 (z_hi: 2, z_lo: 4; z = z_hi * 4 + z_lo), core: 2. Of those that a mesh axis runs over, the one named last changes fastest.
Arguments:
- trajectory: bfloat16 [128, 2, 64, 128], P('tm', None, 'rows'), may hold values from -6 to 6
- observed: float32 [128, 2, 1024], P('tm'), may hold values from -6 to 6
- station_rows: int32 [1024], replicated, may hold values from 0 to 63
- station_cols: int32 [1024], replicated, may hold values from 0 to 127
- step_index: int32 [1], replicated, may hold values from 32 to 223
- w_in: bfloat16 [96, 10, 3, 3], replicated, may hold values from -0.625 to 0.625
- w_mid: bfloat16 [3, 3, 9216], replicated, may hold values from -0.21875 to 0.21875
- w_out: bfloat16 [2, 96, 3, 3], replicated, may hold values from -0.21875 to 0.21875
- noise_gain: float32 [96], replicated, may hold values from -4 to 4
Outputs:
- posterior: float32 [128, 2, 64, 128], P('tm', None, 'rows')
The draws below stay inside these ranges and needn't reach their ends.
All inputs are finite; a program needn't handle non-finite values.
Results may differ from the reference program's by a relative error of at most 0.009.
Values may be sent and summed in bfloat16 or wider, within the bound.
No kernel may reach another device: no remote copies, remote signals or barrier semaphores. Data moves between devices by JAX's collectives and lax.ppermute only.
A program may use at most 64 MiB of HBM per device.

```python
import math
import jax
import jax.numpy as jnp
from jax import lax

HID = 96
NSTEPS = 256
NX = 128
NY = 64
STATES = 128
NOBS = 1024


def plant(drawn, stream_key, least, high):
    index_at = [jax.random.randint(jax.random.fold_in(stream_key, axis), (), 0, length) for axis, length in enumerate(drawn.shape)]
    longest = drawn.shape.index(max(drawn.shape))
    next_to = index_at[:longest] + [(index_at[longest] + 1) % drawn.shape[longest]] + index_at[longest + 1:]
    return drawn.at[tuple(index_at)].set(least).at[tuple(next_to)].set(high)


def levels(own_key, extent, pieces, smallest, largest):
    def one(axis_at, parts):
        steps = jax.random.uniform(jax.random.fold_in(jax.random.fold_in(own_key, 6), axis_at), (parts,), jnp.float32, smallest / len(pieces), largest / len(pieces))
        return jnp.repeat(jnp.exp(steps), extent[axis_at] // parts).reshape((-1,) + (1,) * (len(extent) - axis_at - 1))

    level = one(*pieces[0])
    for cut in pieces[1:]:
        level = level * one(*cut)
    return level


def noise(key, extent, width, most, cuts=(), kind=jnp.bfloat16):
    array = width * jax.random.normal(key, extent, jnp.float32)
    if cuts:
        array = array * levels(key, extent, cuts, -0.22, 0.18)
    return jnp.clip(array, -most, most).astype(kind)


def setup_inputs(seed: int = 0) -> dict:
    splits = jax.random.split(jax.random.key(seed), 10)
    return {
        "trajectory": noise(splits[0], (STATES, 2, NY, NX), 1.0, 6.0, ((0, 128), (2, 4))),
        "observed": noise(splits[1], (STATES, 2, NOBS), 1.0, 6.0, ((0, 128),), jnp.float32),
        "station_rows": plant(jax.random.randint(splits[2], (NOBS,), 0, NY), jax.random.fold_in(splits[2], 1), 0, NY - 1).astype(jnp.int32),
        "station_cols": plant(jax.random.randint(splits[3], (NOBS,), 0, NX), jax.random.fold_in(splits[3], 1), 0, NX - 1).astype(jnp.int32),
        "step_index": jax.random.randint(splits[4], (1,), NSTEPS // 8, NSTEPS - NSTEPS // 8).astype(jnp.int32),
        "w_in": noise(splits[5], (HID, 10, 3, 3), 90 ** -0.5, 0.625),
        "w_mid": noise(splits[6], (3, 3, HID * HID), (9 * HID) ** -0.5, 0.21875),
        "w_out": noise(splits[7], (2, HID, 3, 3), (9 * HID) ** -0.5, 0.21875),
        "noise_gain": noise(splits[8], (HID,), 1.0, 4.0, (), jnp.float32),
    }


def noise_level(step_index):
    phase_time = (step_index[0].astype(jnp.float32) + 0.5) / NSTEPS
    noise_alpha = jnp.cos(0.5 * math.pi * phase_time)
    noise_sigma = jnp.sin(0.5 * math.pi * phase_time)
    obs_kappa = 1.0 + (noise_sigma / noise_alpha) ** 2
    return noise_alpha, noise_sigma, obs_kappa


def conv_full(inputs, weight):
    padded = jnp.pad(inputs.astype(jnp.float32), ((0, 0), (1, 1), (1, 1)), mode="wrap")
    result = lax.conv_general_dilated(padded[None], weight.astype(jnp.float32), (1, 1), "VALID",
                                      dimension_numbers=("NCHW", "OIHW", "NCHW"),
                                      precision=lax.Precision.HIGHEST)
    return result[0]


def adjoint(weight):
    return jnp.transpose(jnp.flip(weight, (2, 3)), (1, 0, 2, 3))


def silu_slope(values):
    logistic = jax.nn.sigmoid(values)
    return logistic * (1.0 + values * (1.0 - logistic))


def reference(trajectory, observed, station_rows, station_cols, step_index, w_in, w_mid, w_out, noise_gain):
    noise_alpha, noise_sigma, obs_kappa = noise_level(step_index)
    mid_kernel = jnp.transpose(w_mid.reshape(3, 3, HID, HID), (2, 3, 0, 1))
    w_in_adj = adjoint(w_in)
    w_mid_adj = adjoint(mid_kernel)
    w_out_adj = adjoint(w_out)
    edge = jnp.zeros((2, 2, NY, NX), jnp.bfloat16)
    padded_traj = jnp.concatenate([edge, trajectory, edge], axis=0)
    shift_bias = (noise_sigma * noise_gain)[:, None, None]

    def window(accrued, position):
        blanket = lax.dynamic_slice_in_dim(padded_traj, position, 5, 0).reshape(10, NY, NX)
        pre_one = conv_full(blanket, w_in) + shift_bias
        hidden_one = jax.nn.silu(pre_one).astype(jnp.bfloat16)
        pre_two = conv_full(hidden_one, mid_kernel)
        hidden_two = (hidden_one.astype(jnp.float32) + jax.nn.silu(pre_two)).astype(jnp.bfloat16)
        noise_pred = conv_full(hidden_two, w_out)
        own_state = blanket[4:6].astype(jnp.float32)
        denoised = (own_state - noise_sigma * noise_pred) / noise_alpha
        picked = denoised[:, station_rows, station_cols]
        obs_row = lax.dynamic_index_in_dim(observed, position, 0, keepdims=False)
        misfit = (obs_row - picked) / obs_kappa
        obs_pull = jnp.zeros((2, NY, NX), jnp.float32).at[:, station_rows, station_cols].add(misfit)
        pull_low = obs_pull.astype(jnp.bfloat16)
        grad_two = conv_full(pull_low, w_out_adj)
        slope_two = (grad_two * silu_slope(pre_two)).astype(jnp.bfloat16)
        grad_one = grad_two + conv_full(slope_two, w_mid_adj)
        slope_one = (grad_one * silu_slope(pre_one)).astype(jnp.bfloat16)
        grad_in = conv_full(slope_one, w_in_adj).reshape(5, 2, NY, NX)
        current = lax.dynamic_slice_in_dim(accrued, position, 5, 0)
        accrued = lax.dynamic_update_slice_in_dim(accrued, current + grad_in, position, 0)
        return accrued, (noise_pred, obs_pull)

    accrued = jnp.zeros((STATES + 4, 2, NY, NX), jnp.float32)
    accrued, (noises, pulls) = lax.scan(window, accrued, jnp.arange(STATES, dtype=jnp.int32))
    summed = accrued[2:STATES + 2]
    return -noises / noise_sigma + (pulls - noise_sigma * summed) / noise_alpha
```

```python
import math

import jax
import jax.numpy as jnp
from jax import lax
from jax.experimental import pallas as pl
from jax.experimental.pallas import tpu as pltpu
from jax.sharding import PartitionSpec as P

NSTEPS = 256
HID = 96
WIDTH = 128
OWN = 16
REACH = 2
WINDOWS = 2 * REACH + 1
SPAN = 24
BLOCK = 6 * OWN
PULL = 4 * SPAN
ONE = BLOCK + PULL
THREE = 3 * BLOCK + PULL
F32 = jnp.float32
BF16 = jnp.bfloat16


def noise_level(step_index):
    phase_time = (step_index[0].astype(F32) + 0.5) / NSTEPS
    noise_alpha = jnp.cos(0.5 * math.pi * phase_time)
    noise_sigma = jnp.sin(0.5 * math.pi * phase_time)
    obs_kappa = 1.0 + (noise_sigma / noise_alpha) ** 2
    return noise_alpha, noise_sigma, obs_kappa


def station_kernel(first_ref, rows_ref, cols_ref, obs_ref, pull_ref, count_ref):
    stations = rows_ref.shape[1]
    offset = rows_ref[...] - first_ref[0]
    offset = jnp.where(offset < 0, offset + 64, offset)
    offset = jnp.where(offset >= 64, offset - 64, offset)
    place = lax.broadcasted_iota(jnp.int32, (SPAN, stations), 0)
    hit = place == jnp.broadcast_to(offset, (SPAN, stations))
    parts = []
    for f in range(2):
        values = obs_ref[f : f + 1, :]
        left = values
        for _ in range(3):
            part = left.astype(BF16).astype(F32)
            left = left - part
            parts.append(jnp.where(hit, jnp.broadcast_to(part, hit.shape), 0.0))
    parts.append(jnp.where(hit, 1.0, 0.0))
    left_side = jnp.concatenate(parts, axis=0).astype(BF16)
    column = lax.broadcasted_iota(jnp.int32, (WIDTH, stations), 0)
    at_column = jnp.where(
        column == jnp.broadcast_to(cols_ref[...], (WIDTH, stations)), 1.0, 0.0
    ).astype(BF16)
    sums = lax.dot_general(
        left_side, at_column, (((1,), (1,)), ((), ())), preferred_element_type=F32
    )
    total = jnp.concatenate(
        [
            sums[3 * SPAN * f : 3 * SPAN * f + SPAN]
            + sums[3 * SPAN * f + SPAN : 3 * SPAN * f + 2 * SPAN]
            + sums[3 * SPAN * f + 2 * SPAN : 3 * SPAN * f + 3 * SPAN]
            for f in range(2)
        ],
        axis=0,
    )
    high = total.astype(BF16)
    pull_ref[: 2 * SPAN, :] = high
    pull_ref[2 * SPAN :, :] = (total - high.astype(F32)).astype(BF16)
    count_ref[...] = sums[6 * SPAN : 7 * SPAN]


def logistic(values):
    return 0.5 + 0.5 * jnp.tanh(0.5 * values)


def rolled(values, shift):
    if shift == 0:
        return values
    return jnp.concatenate(
        [
            pltpu.roll(values[:, k : k + WIDTH], (-shift) % WIDTH, 1)
            for k in range(0, values.shape[1], WIDTH)
        ],
        axis=1,
    )


def store_shifted(ref, start, values):
    for b in range(3):
        moved = rolled(values, b - 1).astype(BF16)
        for k in range(2):
            ref[pl.ds(pl.multiple_of(start + (3 * k + b) * HID, 16), HID), :] = moved[
                :, k * WIDTH : (k + 1) * WIDTH
            ]


def two_rows(ref, start, slab, depth):
    return jnp.concatenate(
        [
            ref[pl.ds(pl.multiple_of(start + k * slab, 8), depth), :].astype(BF16)
            for k in range(2)
        ],
        axis=1,
    )


def dot(left, right):
    return lax.dot_general(
        left, right, (((1,), (0,)), ((), ())), preferred_element_type=F32
    )


def folded(product):
    return rolled(product[0:8], -1) + product[8:16] + rolled(product[16:24], 1)


def score_kernel(
    scalars_ref,
    own_ref,
    before_ref,
    after_ref,
    far_before_ref,
    far_after_ref,
    count_ref,
    bias_ref,
    w_in_ref,
    w_mid_ref,
    w_out_ref,
    w_out_adj_ref,
    w_back_ref,
    w_in_adj_ref,
    out_ref,
    moved,
    sums,
    blanket,
    hidden,
    slope_one,
    slope_two,
    folds,
    pull_slabs,
    back,
    grads,
    kept,
):
    noise_alpha = scalars_ref[0]
    noise_sigma = scalars_ref[1]
    obs_kappa = scalars_ref[2]
    over_alpha = 1.0 / noise_alpha
    over_kappa = 1.0 / obs_kappa

    blanket[...] = jnp.zeros_like(blanket)
    folds[...] = jnp.zeros_like(folds)
    pull_slabs[...] = jnp.zeros_like(pull_slabs)
    grads[...] = jnp.zeros_like(grads)

    places = (
        (far_before_ref, 0),
        (far_before_ref, BLOCK),
        (far_before_ref, 2 * BLOCK),
        (before_ref, 0),
        (own_ref, 0),
        (after_ref, 0),
        (far_after_ref, 0),
        (far_after_ref, BLOCK),
        (far_after_ref, 2 * BLOCK),
    )
    for s, (ref, start) in enumerate(places):
        inside = scalars_ref[3 + s]
        for f in range(2):
            rows = [
                ref[pl.ds(start + OWN * (2 * block + f), OWN), :].astype(F32)
                for block in range(3)
            ]
            field = inside * jnp.concatenate(
                [rows[0][8:], rows[1], rows[2][:8]], axis=0
            )
            for b in range(3):
                moved[b, 2 * s + f, :, :] = rolled(field, b - 1)

    for w, (ref, start) in enumerate(
        (
            (far_before_ref, 3 * BLOCK),
            (before_ref, BLOCK),
            (own_ref, BLOCK),
            (after_ref, BLOCK),
            (far_after_ref, 3 * BLOCK),
        )
    ):
        sums[w, :, :] = ref[pl.ds(start, 2 * SPAN), :].astype(F32) + ref[
            pl.ds(start + 2 * SPAN, 2 * SPAN), :
        ].astype(F32)

    def window(w, _):
        inside = scalars_ref[3 + REACH + w]
        for b in range(3):
            for channel in range(2 * WINDOWS):
                blanket[pl.ds(16 * b + channel, 32, stride=48), :] = moved[
                    b, 2 * w + channel, :, :
                ]

        def first_layer(p, _):
            bias = bias_ref[...]
            values = dot(w_in_ref[...], two_rows(blanket, 48 * (2 * p + 2), 48, 144))
            values = values + jnp.concatenate([bias, bias], axis=1)
            gate = logistic(values)
            result = values * gate
            slope = gate + result * (1.0 - gate)
            store_shifted(hidden, 6 * HID * p, result)
            for k in range(2):
                slope_one[pl.ds(pl.multiple_of(HID * (2 * p + k), 8), HID), :] = slope[
                    :, k * WIDTH : (k + 1) * WIDTH
                ]
            return 0

        lax.fori_loop(0, 13, first_layer, 0)

        def second_layer(q, _):
            values = dot(w_mid_ref[...], two_rows(hidden, 6 * HID * q, 3 * HID, 9 * HID))
            gate = logistic(values)
            result = values * gate
            slope = gate + result * (1.0 - gate)
            residual = jnp.concatenate(
                [
                    hidden[pl.ds(pl.multiple_of(3 * HID * (2 * q + 1 + k) + HID, 16), HID), :]
                    for k in range(2)
                ],
                axis=1,
            )
            high = (residual.astype(F32) + result).astype(BF16)
            fold = folded(dot(w_out_ref[...], high))
            for k in range(2):
                slope_two[pl.ds(pl.multiple_of(HID * (2 * q + k), 8), HID), :] = slope[
                    :, k * WIDTH : (k + 1) * WIDTH
                ]
                folds[pl.ds(pl.multiple_of(8 * (2 * q + k), 8), 8), :] = fold[
                    :, k * WIDTH : (k + 1) * WIDTH
                ]
            return 0

        lax.fori_loop(0, 12, second_layer, 0)

        for f in range(2):
            noise_pred = (
                folds[pl.ds(f, SPAN, stride=8), :]
                + folds[pl.ds(8 + 2 + f, SPAN, stride=8), :]
                + folds[pl.ds(16 + 4 + f, SPAN, stride=8), :]
            )
            state = moved[1, 2 * w + 2 * REACH + f, pl.ds(5, SPAN), :]
            denoised = (state - noise_sigma * noise_pred) * over_alpha
            pull = (
                sums[w, pl.ds(SPAN * f, SPAN), :] - count_ref[...] * denoised
            ) * over_kappa
            for b in range(3):
                pull_slabs[pl.ds(2 * b + f, SPAN, stride=16), :] = rolled(pull, b - 1)

            @pl.when(w == REACH)
            def _():
                kept[f, :, :] = noise_pred
                kept[2 + f, :, :] = pull

        def second_back(t, _):
            gradient = dot(w_out_adj_ref[...], two_rows(pull_slabs, 32 * t, 16, 48))
            slope = jnp.concatenate(
                [
                    slope_two[pl.ds(pl.multiple_of(HID * (2 * t + 2 + k), 8), HID), :]
                    for k in range(2)
                ],
                axis=1,
            )
            store_shifted(back, 6 * HID * t, gradient * slope)
            return 0

        lax.fori_loop(0, 10, second_back, 0)

        def first_back(u, _):
            operand = jnp.concatenate(
                [
                    two_rows(back, 6 * HID * u, 3 * HID, 9 * HID),
                    two_rows(pull_slabs, 16 * (2 * u + 1), 16, 48),
                ],
                axis=0,
            )
            gradient = dot(w_back_ref[...], operand)
            slope = jnp.concatenate(
                [
                    slope_one[pl.ds(pl.multiple_of(HID * (2 * u + 4 + k), 8), HID), :]
                    for k in range(2)
                ],
                axis=1,
            )
            fold = inside * folded(dot(w_in_adj_ref[w], (gradient * slope).astype(BF16)))
            for k in range(2):
                at = pl.ds(pl.multiple_of(8 * (2 * u + k), 8), 8)
                grads[at, :] = grads[at, :] + fold[:, k * WIDTH : (k + 1) * WIDTH]
            return 0

        lax.fori_loop(0, 9, first_back, 0)
        return 0

    lax.fori_loop(0, WINDOWS, window, 0)

    for f in range(2):
        summed = (
            grads[pl.ds(f, OWN, stride=8), :]
            + grads[pl.ds(8 + 2 + f, OWN, stride=8), :]
            + grads[pl.ds(16 + 4 + f, OWN, stride=8), :]
        )
        noise_pred = kept[f, pl.ds(3, OWN), :]
        pull = kept[2 + f, pl.ds(3, OWN), :]
        out_ref[f, :, :] = -noise_pred / noise_sigma + (
            pull - noise_sigma * summed
        ) * over_alpha


def padded(array, axis, size):
    pads = [(0, 0)] * array.ndim
    pads[axis] = (0, size - array.shape[axis])
    return jnp.pad(array, pads)


def matrices(w_in, w_mid, w_out):
    taps = w_mid.reshape(9, HID, HID)
    mid = jnp.transpose(taps, (1, 0, 2)).reshape(HID, 9 * HID)
    mid_adj = jnp.transpose(taps[::-1], (2, 0, 1)).reshape(HID, 9 * HID)
    first = padded(jnp.transpose(w_in, (0, 2, 3, 1)), 3, 16).reshape(HID, 144)
    last = padded(
        jnp.transpose(w_out, (3, 2, 0, 1)).reshape(3, 6, HID), 1, 8
    ).reshape(24, HID)
    flipped_out = w_out[:, :, ::-1, ::-1]
    last_adj = padded(
        jnp.transpose(flipped_out, (1, 2, 3, 0)).reshape(HID, 3, 6), 2, 16
    ).reshape(HID, 48)
    flipped_in = w_in[:, :, ::-1, ::-1].reshape(HID, WINDOWS, 2, 3, 3)[:, ::-1]
    first_adj = padded(
        jnp.transpose(flipped_in, (1, 4, 3, 2, 0)).reshape(WINDOWS, 3, 6, HID), 2, 8
    ).reshape(WINDOWS, 24, HID)
    return first, mid, last, last_adj, jnp.concatenate([mid_adj, last_adj], axis=1), first_adj


def on_device(
    trajectory, observed, station_rows, station_cols, step_index, w_in, w_mid, w_out, noise_gain
):
    place = lax.axis_index("tm")
    part = lax.axis_index("rows")
    count = lax.axis_size("tm")
    noise_alpha, noise_sigma, obs_kappa = noise_level(step_index)
    own_state = trajectory[0]

    far = lax.ppermute(own_state, "rows", [(1, 2), (2, 1), (3, 0), (0, 3)])
    near = lax.ppermute(own_state, "rows", [(0, 1), (1, 0), (2, 3), (3, 2)])

    vmem = pl.BlockSpec(memory_space=pltpu.VMEM)
    smem = pl.BlockSpec(memory_space=pltpu.SMEM)
    pulls, counts = pl.pallas_call(
        station_kernel,
        out_shape=(
            jax.ShapeDtypeStruct((PULL, WIDTH), BF16),
            jax.ShapeDtypeStruct((SPAN, WIDTH), F32),
        ),
        in_specs=[smem, vmem, vmem, vmem],
        out_specs=(vmem, vmem),
        cost_estimate=pl.CostEstimate(flops=40_000_000, bytes_accessed=50_000, transcendentals=0),
        name="stations",
    )(
        (part * OWN - 3).reshape(1).astype(jnp.int32),
        station_rows.reshape(1, -1),
        station_cols.reshape(1, -1),
        observed[0],
    )
    weights = matrices(w_in, w_mid, w_out)
    bias = jnp.broadcast_to((noise_sigma * noise_gain)[:, None], (HID, WIDTH))
    states = place + jnp.arange(-2 * REACH, 2 * REACH + 1)
    inside = ((states >= 0) & (states < count)).astype(F32)
    scalars = jnp.concatenate(
        [jnp.stack([noise_alpha, noise_sigma, obs_kappa]), inside, jnp.zeros(4, F32)]
    )

    even = part % 2 == 0
    above = jnp.where(even, far, near)
    below = jnp.where(even, near, far)
    own = jnp.concatenate([above, own_state, below], axis=0).reshape(BLOCK, WIDTH)
    own = jnp.concatenate([own, pulls], axis=0)

    def ring(value, steps):
        return lax.ppermute(value, "tm", [(k, (k + steps) % count) for k in range(count)])

    before = ring(own, 1)
    after = ring(own, -1)
    three = jnp.concatenate([before[:BLOCK], own[:BLOCK], after[:BLOCK]], axis=0)
    far_before = ring(jnp.concatenate([three, after[BLOCK:]], axis=0), 3)
    far_after = ring(jnp.concatenate([three, before[BLOCK:]], axis=0), -3)

    posterior = pl.pallas_call(
        score_kernel,
        out_shape=jax.ShapeDtypeStruct((2, OWN, WIDTH), F32),
        in_specs=[smem] + [vmem] * 13,
        out_specs=vmem,
        scratch_shapes=[
            pltpu.VMEM((3, 18, 32, WIDTH), F32),
            pltpu.VMEM((WINDOWS, 2 * SPAN, WIDTH), F32),
            pltpu.VMEM((32 * 48, WIDTH), F32),
            pltpu.VMEM((26 * 3 * HID, WIDTH), BF16),
            pltpu.VMEM((26 * HID, WIDTH), F32),
            pltpu.VMEM((24 * HID, WIDTH), F32),
            pltpu.VMEM((32 * 8, WIDTH), F32),
            pltpu.VMEM((SPAN * 16, WIDTH), F32),
            pltpu.VMEM((20 * 3 * HID, WIDTH), BF16),
            pltpu.VMEM((18 * 8, WIDTH), F32),
            pltpu.VMEM((4, SPAN, WIDTH), F32),
        ],
        compiler_params=pltpu.CompilerParams(vmem_limit_bytes=32 * 1024 * 1024),
        cost_estimate=pl.CostEstimate(
            flops=5_000_000_000, bytes_accessed=1_000_000, transcendentals=1_000_000
        ),
        name="score",
    )(
        scalars,
        own,
        before,
        after,
        far_before,
        far_after,
        counts,
        bias,
        *weights,
    )
    return posterior[None]


def solution(mesh):
    return jax.shard_map(
        on_device,
        mesh=mesh,
        in_specs=(
            P("tm", None, "rows", None),
            P("tm", None, None),
            P(),
            P(),
            P(),
            P(),
            P(),
            P(),
            P(),
        ),
        out_specs=P("tm", None, "rows", None),
        check_vma=False,
    )
```

```python
import math

import jax
import jax.numpy as jnp
from jax import lax
from jax.experimental import pallas as pl
from jax.experimental.pallas import tpu as pltpu
from jax.sharding import PartitionSpec as P

NSTEPS = 256
HID = 96
WIDTH = 128
OWN = 16
REACH = 2
WINDOWS = 2 * REACH + 1
SPAN = 24
EDGE = 8
BLOCK = 2 * OWN + 4 * EDGE
STATIONS = 1024
SEEN = 4 * STATIONS // WIDTH
ONE = BLOCK + SEEN
THREE = 3 * BLOCK + SEEN
PLAN = ((2, 99), (24, 99), (2, 99), (18, 99))
F32 = jnp.float32
BF16 = jnp.bfloat16


def noise_level(step_index):
    phase_time = (step_index[0].astype(F32) + 0.5) / NSTEPS
    noise_alpha = jnp.cos(0.5 * math.pi * phase_time)
    noise_sigma = jnp.sin(0.5 * math.pi * phase_time)
    obs_kappa = 1.0 + (noise_sigma / noise_alpha) ** 2
    return noise_alpha, noise_sigma, obs_kappa


def station_sums(first, rows_ref, cols_ref, seen):
    left_side, at_column = [], []
    chunks = STATIONS // WIDTH
    for chunk in range(chunks):
        offset = rows_ref[chunk : chunk + 1, :] - first
        offset = jnp.where(offset < 0, offset + 64, offset)
        offset = jnp.where(offset >= 64, offset - 64, offset)
        place = lax.broadcasted_iota(jnp.int32, (SPAN, WIDTH), 0)
        hit = place == jnp.broadcast_to(offset, (SPAN, WIDTH))
        parts = [jnp.where(hit, 1.0, 0.0)]
        for values in seen:
            for part in range(4):
                row = values[chunks * part + chunk : chunks * part + chunk + 1, :]
                parts.append(jnp.where(hit, jnp.broadcast_to(row, (SPAN, WIDTH)), 0.0))
        left_side.append(jnp.concatenate(parts, axis=0).astype(BF16))
        column = lax.broadcasted_iota(jnp.int32, (WIDTH, WIDTH), 0)
        at = jnp.broadcast_to(cols_ref[chunk : chunk + 1, :], (WIDTH, WIDTH))
        at_column.append(jnp.where(column == at, 1.0, 0.0).astype(BF16))
    sums = lax.dot_general(
        jnp.concatenate(left_side, axis=1),
        jnp.concatenate(at_column, axis=1),
        (((1,), (1,)), ((), ())),
        preferred_element_type=F32,
    )
    results = []
    for k in range(len(seen)):
        start = SPAN * (4 * k + 1)
        results.append(
            sums[start : start + 2 * SPAN] + sums[start + 2 * SPAN : start + 4 * SPAN]
        )
    return results + [sums[:SPAN]]


def logistic(values):
    return 0.5 + 0.5 * jnp.tanh(0.5 * values)


def rolled(values, shift):
    if shift == 0:
        return values
    return jnp.concatenate(
        [
            pltpu.roll(values[:, k : k + WIDTH], (-shift) % WIDTH, 1)
            for k in range(0, values.shape[1], WIDTH)
        ],
        axis=1,
    )


def store_shifted(ref, start, values):
    low = values.astype(BF16)
    for b in range(3):
        moved = rolled(low, b - 1)
        for k in range(values.shape[1] // WIDTH):
            ref[pl.ds(pl.multiple_of(start + (3 * k + b) * HID, 16), HID), :] = moved[
                :, k * WIDTH : (k + 1) * WIDTH
            ]


def store_rows(ref, start, slab, values):
    for k in range(values.shape[1] // WIDTH):
        ref[pl.ds(pl.multiple_of(start + k * slab, 8), slab), :] = values[
            :, k * WIDTH : (k + 1) * WIDTH
        ]


def side_by_side(ref, start, slab, depth, rows):
    return jnp.concatenate(
        [
            ref[pl.ds(pl.multiple_of(start + k * slab, 8), depth), :].astype(BF16)
            for k in range(rows)
        ],
        axis=1,
    )


def wide(ref, start, slab, rows):
    return jnp.concatenate(
        [ref[pl.ds(pl.multiple_of(start + k * slab, 8), slab), :] for k in range(rows)], axis=1
    )


def over_rows(body, total, rows, unroll):
    steps = total // rows

    def step(k, carry):
        body(k * rows, rows)
        return carry

    if unroll >= steps:
        for k in range(steps):
            body(k * rows, rows)
    else:
        lax.fori_loop(0, steps, step, 0, unroll=unroll)
    if total % rows:
        body(steps * rows, total % rows)


def dot(left, right):
    return lax.dot_general(
        left, right, (((1,), (0,)), ((), ())), preferred_element_type=F32
    )


def folded(product):
    return rolled(product[0:8], -1) + product[8:16] + rolled(product[16:24], 1)


def score_kernel(
    scalars_ref,
    first_ref,
    rows_ref,
    cols_ref,
    seen_ref,
    near_after_ref,
    near_before_ref,
    far_before_ref,
    far_after_ref,
    bias_ref,
    w_in_ref,
    w_mid_ref,
    w_out_ref,
    w_out_adj_ref,
    w_back_ref,
    w_in_adj_ref,
    out_ref,
    moved,
    sums,
    count,
    blanket,
    hidden,
    slope_one,
    slope_two,
    folds,
    pull_slabs,
    back,
    grads,
    kept,
):
    noise_alpha = scalars_ref[0]
    noise_sigma = scalars_ref[1]
    obs_kappa = scalars_ref[2]
    over_alpha = 1.0 / noise_alpha
    over_kappa = 1.0 / obs_kappa

    blanket[...] = jnp.zeros_like(blanket)
    folds[...] = jnp.zeros_like(folds)
    pull_slabs[...] = jnp.zeros_like(pull_slabs)
    grads[...] = jnp.zeros_like(grads)

    places = (
        (far_before_ref, 0),
        (far_before_ref, BLOCK),
        (far_before_ref, 2 * BLOCK),
        (near_after_ref, 0),
        (near_after_ref, BLOCK),
        (near_after_ref, 2 * BLOCK),
        (far_after_ref, 0),
        (far_after_ref, BLOCK),
        (far_after_ref, 2 * BLOCK),
    )
    for s, (ref, start) in enumerate(places):
        inside = scalars_ref[3 + s]
        above = ref[pl.ds(start + 2 * OWN, 2 * EDGE), :].astype(F32)
        below = ref[pl.ds(start + 2 * OWN + 2 * EDGE, 2 * EDGE), :].astype(F32)
        for f in range(2):
            rows = ref[pl.ds(start + OWN * f, OWN), :].astype(F32)
            edge = slice(EDGE * f, EDGE * (f + 1))
            field = inside * jnp.concatenate([above[edge], rows, below[edge]], axis=0)
            for b in range(3):
                moved[b, 2 * s + f, :, :] = rolled(field, b - 1)

    seen = [
        ref[pl.ds(start, SEEN), :].astype(F32)
        for ref, start in (
            (far_before_ref, 3 * BLOCK),
            (near_before_ref, 3 * BLOCK),
            (seen_ref, 0),
            (near_after_ref, 3 * BLOCK),
            (far_after_ref, 3 * BLOCK),
        )
    ]
    *totals, stations = station_sums(first_ref[0], rows_ref, cols_ref, seen)
    for k in range(WINDOWS):
        sums[k, :, :] = totals[k]
    count[...] = stations

    def window(w, _):
        inside = scalars_ref[3 + REACH + w]
        for b in range(3):
            for channel in range(2 * WINDOWS):
                blanket[pl.ds(16 * b + channel, 32, stride=48), :] = moved[
                    b, 2 * w + channel, :, :
                ]

        def first_layer(p, rows):
            values = dot(w_in_ref[...], side_by_side(blanket, 48 * (p + 2), 48, 144, rows))
            values = values + jnp.concatenate([bias_ref[...]] * rows, axis=1)
            gate = logistic(values)
            result = values * gate
            store_shifted(hidden, 3 * HID * p, result)
            store_rows(slope_one, HID * p, HID, gate + result * (1.0 - gate))

        over_rows(first_layer, 26, *PLAN[0])

        def second_layer(q, rows):
            operand = side_by_side(hidden, 3 * HID * q, 3 * HID, 9 * HID, rows)
            values = dot(w_mid_ref[...], operand)
            gate = logistic(values)
            result = values * gate
            residual = side_by_side(hidden, 3 * HID * (q + 1) + HID, 3 * HID, HID, rows)
            high = (residual.astype(F32) + result).astype(BF16)
            store_rows(slope_two, HID * q, HID, gate + result * (1.0 - gate))
            store_rows(folds, 8 * q, 8, folded(dot(w_out_ref[...], high)))

        over_rows(second_layer, 24, *PLAN[1])

        for f in range(2):
            noise_pred = (
                folds[pl.ds(f, SPAN, stride=8), :]
                + folds[pl.ds(8 + 2 + f, SPAN, stride=8), :]
                + folds[pl.ds(16 + 4 + f, SPAN, stride=8), :]
            )
            state = moved[1, 2 * w + 2 * REACH + f, pl.ds(5, SPAN), :]
            denoised = (state - noise_sigma * noise_pred) * over_alpha
            pull = (
                sums[w, pl.ds(SPAN * f, SPAN), :] - count[...] * denoised
            ) * over_kappa
            for b in range(3):
                pull_slabs[pl.ds(2 * b + f, SPAN, stride=16), :] = rolled(pull, b - 1)

            @pl.when(w == REACH)
            def _():
                kept[f, :, :] = noise_pred
                kept[2 + f, :, :] = pull

        def second_back(t, rows):
            operand = side_by_side(pull_slabs, 16 * t, 16, 48, rows)
            slope = wide(slope_two, HID * (t + 2), HID, rows)
            store_shifted(back, 3 * HID * t, dot(w_out_adj_ref[...], operand) * slope)

        over_rows(second_back, 20, *PLAN[2])

        def first_back(u, rows):
            operand = jnp.concatenate(
                [
                    side_by_side(back, 3 * HID * u, 3 * HID, 9 * HID, rows),
                    side_by_side(pull_slabs, 16 * (u + 1), 16, 48, rows),
                ],
                axis=0,
            )
            slope = wide(slope_one, HID * (u + 4), HID, rows)
            low = (dot(w_back_ref[...], operand) * slope).astype(BF16)
            fold = inside * folded(dot(w_in_adj_ref[w], low))
            for k in range(rows):
                at = pl.ds(pl.multiple_of(8 * (u + k), 8), 8)
                grads[at, :] = grads[at, :] + fold[:, k * WIDTH : (k + 1) * WIDTH]

        over_rows(first_back, 18, *PLAN[3])
        return 0

    lax.fori_loop(0, WINDOWS, window, 0)

    for f in range(2):
        summed = (
            grads[pl.ds(f, OWN, stride=8), :]
            + grads[pl.ds(8 + 2 + f, OWN, stride=8), :]
            + grads[pl.ds(16 + 4 + f, OWN, stride=8), :]
        )
        noise_pred = kept[f, pl.ds(3, OWN), :]
        pull = kept[2 + f, pl.ds(3, OWN), :]
        out_ref[f, :, :] = -noise_pred / noise_sigma + (
            pull - noise_sigma * summed
        ) * over_alpha


def score(*operands):
    vmem = pl.BlockSpec(memory_space=pltpu.VMEM)
    smem = pl.BlockSpec(memory_space=pltpu.SMEM)
    return pl.pallas_call(
        score_kernel,
        out_shape=jax.ShapeDtypeStruct((2, OWN, WIDTH), F32),
        in_specs=[smem, smem] + [vmem] * 14,
        out_specs=vmem,
        scratch_shapes=[
            pltpu.VMEM((3, 18, 32, WIDTH), F32),
            pltpu.VMEM((WINDOWS, 2 * SPAN, WIDTH), F32),
            pltpu.VMEM((SPAN, WIDTH), F32),
            pltpu.VMEM((32 * 48, WIDTH), F32),
            pltpu.VMEM((26 * 3 * HID, WIDTH), BF16),
            pltpu.VMEM((26 * HID, WIDTH), F32),
            pltpu.VMEM((24 * HID, WIDTH), F32),
            pltpu.VMEM((32 * 8, WIDTH), F32),
            pltpu.VMEM((SPAN * 16, WIDTH), F32),
            pltpu.VMEM((20 * 3 * HID, WIDTH), BF16),
            pltpu.VMEM((18 * 8, WIDTH), F32),
            pltpu.VMEM((4, SPAN, WIDTH), F32),
        ],
        compiler_params=pltpu.CompilerParams(vmem_limit_bytes=32 * 1024 * 1024),
        cost_estimate=pl.CostEstimate(
            flops=5_000_000_000, bytes_accessed=1_000_000, transcendentals=1_000_000
        ),
        name="score",
    )(
        *operands
    )


def padded(array, axis, size):
    pads = [(0, 0)] * array.ndim
    pads[axis] = (0, size - array.shape[axis])
    return jnp.pad(array, pads)


def matrices(w_in, w_mid, w_out):
    taps = w_mid.reshape(9, HID, HID)
    mid = jnp.transpose(taps, (1, 0, 2)).reshape(HID, 9 * HID)
    mid_adj = jnp.transpose(taps[::-1], (2, 0, 1)).reshape(HID, 9 * HID)
    first = padded(jnp.transpose(w_in, (0, 2, 3, 1)), 3, 16).reshape(HID, 144)
    last = padded(
        jnp.transpose(w_out, (3, 2, 0, 1)).reshape(3, 6, HID), 1, 8
    ).reshape(24, HID)
    flipped_out = w_out[:, :, ::-1, ::-1]
    last_adj = padded(
        jnp.transpose(flipped_out, (1, 2, 3, 0)).reshape(HID, 3, 6), 2, 16
    ).reshape(HID, 48)
    flipped_in = w_in[:, :, ::-1, ::-1].reshape(HID, WINDOWS, 2, 3, 3)[:, ::-1]
    first_adj = padded(
        jnp.transpose(flipped_in, (1, 4, 3, 2, 0)).reshape(WINDOWS, 3, 6, HID), 2, 8
    ).reshape(WINDOWS, 24, HID)
    return first, mid, last, last_adj, jnp.concatenate([mid_adj, last_adj], axis=1), first_adj


def on_device(
    trajectory, observed, station_rows, station_cols, step_index, w_in, w_mid, w_out, noise_gain
):
    place = lax.axis_index("tm")
    part = lax.axis_index("rows")
    count = lax.axis_size("tm")
    noise_alpha, noise_sigma, obs_kappa = noise_level(step_index)
    own_state = trajectory[0]

    far = lax.ppermute(own_state, "rows", [(1, 2), (2, 1), (3, 0), (0, 3)])
    near = lax.ppermute(own_state, "rows", [(0, 1), (1, 0), (2, 3), (3, 2)])
    high = observed[0].astype(BF16)
    low = (observed[0] - high.astype(F32)).astype(BF16)
    seen = jnp.concatenate([high, low], axis=0).reshape(SEEN, WIDTH)
    even = part % 2 == 0
    above = jnp.where(even, far, near)[:, OWN - EDGE :].reshape(2 * EDGE, WIDTH)
    below = jnp.where(even, near, far)[:, :EDGE].reshape(2 * EDGE, WIDTH)
    own = jnp.concatenate([own_state.reshape(2 * OWN, WIDTH), above, below, seen], axis=0)

    def ring(value, steps):
        return lax.ppermute(value, "tm", [(k, (k + steps) % count) for k in range(count)])

    before = ring(own, 1)
    after = ring(own, -1)
    own, w_mid = lax.optimization_barrier((own, w_mid))
    first, mid, last, last_adj, back, first_adj = matrices(w_in, w_mid, w_out)
    bias = jnp.broadcast_to((noise_sigma * noise_gain)[:, None], (HID, WIDTH))
    states = place + jnp.arange(-2 * REACH, 2 * REACH + 1)
    inside = ((states >= 0) & (states < count)).astype(F32)
    scalars = jnp.concatenate(
        [jnp.stack([noise_alpha, noise_sigma, obs_kappa]), inside, jnp.zeros(4, F32)]
    )

    three = jnp.concatenate([before[:BLOCK], own[:BLOCK], after[:BLOCK]], axis=0)
    near_after = jnp.concatenate([three, after[BLOCK:]], axis=0)
    near_before = jnp.concatenate([three, before[BLOCK:]], axis=0)
    far_before = ring(near_after, 3)
    far_after = ring(near_before, -3)

    posterior = score(
        scalars,
        (part * OWN - 3).reshape(1).astype(jnp.int32),
        station_rows.reshape(-1, WIDTH),
        station_cols.reshape(-1, WIDTH),
        seen,
        near_after,
        near_before,
        far_before,
        far_after,
        bias,
        first,
        mid,
        last,
        last_adj,
        back,
        first_adj,
    )
    return posterior[None]


def solution(mesh):
    return jax.shard_map(
        on_device,
        mesh=mesh,
        in_specs=(
            P("tm", None, "rows", None),
            P("tm", None, None),
            P(),
            P(),
            P(),
            P(),
            P(),
            P(),
            P(),
        ),
        out_specs=P("tm", None, "rows", None),
        check_vma=False,
    )
```

```python
import math

import jax
import jax.numpy as jnp
from jax import lax
from jax.experimental import pallas as pl
from jax.experimental.pallas import tpu as pltpu
from jax.sharding import PartitionSpec as P

NSTEPS = 256
HID = 96
WIDTH = 128
OWN = 16
REACH = 2
WINDOWS = 2 * REACH + 1
SPAN = 24
EDGE = 8
BLOCK = 2 * OWN + 4 * EDGE
STATIONS = 1024
SEEN = 4 * STATIONS // WIDTH
ONE = BLOCK + SEEN
THREE = 3 * ONE
ORDER = tuple((step, at - step) for at in range(WINDOWS + 5) for step in range(5) if 0 <= at - step < WINDOWS)
F32 = jnp.float32
BF16 = jnp.bfloat16


def noise_level(step_index):
    phase_time = (step_index[0].astype(F32) + 0.5) / NSTEPS
    noise_alpha = jnp.cos(0.5 * math.pi * phase_time)
    noise_sigma = jnp.sin(0.5 * math.pi * phase_time)
    obs_kappa = 1.0 + (noise_sigma / noise_alpha) ** 2
    return noise_alpha, noise_sigma, obs_kappa


def station_sums(first, stations_ref, seen):
    left_side, at_column = [], []
    chunks = STATIONS // WIDTH
    for chunk in range(chunks):
        offset = stations_ref[chunk : chunk + 1, :] - first
        offset = jnp.where(offset < 0, offset + 64, offset)
        offset = jnp.where(offset >= 64, offset - 64, offset)
        place = lax.broadcasted_iota(jnp.int32, (SPAN, WIDTH), 0)
        hit = place == jnp.broadcast_to(offset, (SPAN, WIDTH))
        parts = [jnp.where(hit, 1.0, 0.0)]
        for values in seen:
            for part in range(4):
                row = values[chunks * part + chunk : chunks * part + chunk + 1, :]
                parts.append(jnp.where(hit, jnp.broadcast_to(row, (SPAN, WIDTH)), 0.0))
        left_side.append(jnp.concatenate(parts, axis=0).astype(BF16))
        column = lax.broadcasted_iota(jnp.int32, (WIDTH, WIDTH), 0)
        at = stations_ref[chunks + chunk : chunks + chunk + 1, :]
        at = jnp.broadcast_to(at, (WIDTH, WIDTH))
        at_column.append(jnp.where(column == at, 1.0, 0.0).astype(BF16))
    sums = lax.dot_general(
        jnp.concatenate(left_side, axis=1),
        jnp.concatenate(at_column, axis=1),
        (((1,), (1,)), ((), ())),
        preferred_element_type=F32,
    )
    results = []
    for k in range(len(seen)):
        start = SPAN * (4 * k + 1)
        results.append(
            sums[start : start + 2 * SPAN] + sums[start + 2 * SPAN : start + 4 * SPAN]
        )
    return results + [sums[:SPAN]]


def logistic(values):
    return 0.5 + 0.5 * jnp.tanh(0.5 * values)


def rolled(values, shift):
    if shift == 0:
        return values
    return jnp.concatenate(
        [
            pltpu.roll(values[:, k : k + WIDTH], (-shift) % WIDTH, 1)
            for k in range(0, values.shape[1], WIDTH)
        ],
        axis=1,
    )


def store_shifted(ref, start, step, values):
    low = values.astype(BF16)
    for b in range(3):
        moved = rolled(low, b - 1)
        for k in range(values.shape[1] // WIDTH):
            ref[pl.ds((3 * (start + step * k) + b) * HID, HID), :] = moved[
                :, k * WIDTH : (k + 1) * WIDTH
            ]


def side_by_side(ref, start, step, depth, count):
    return jnp.concatenate(
        [ref[pl.ds(start + k * step, depth), :] for k in range(count)], axis=1
    )


def dot(left, right):
    return lax.dot_general(
        left, right, (((1,), (0,)), ((), ())), preferred_element_type=F32
    )


def folded(product):
    return rolled(product[0:8], -1) + product[8:16] + rolled(product[16:24], 1)


def score_kernel(
    scalars_ref,
    first_ref,
    stations_ref,
    near_ref,
    far_before_ref,
    far_after_ref,
    end_ref,
    bias_ref,
    w_in_ref,
    w_mid_ref,
    w_out_ref,
    w_out_adj_ref,
    w_back_ref,
    w_in_adj_ref,
    out_ref,
    moved,
    sums,
    count,
    blanket,
    hidden,
    slope_one,
    slope_two,
    folds,
    pull_slabs,
    back,
    slopes,
    grads,
    kept,
):
    noise_alpha = scalars_ref[0]
    noise_sigma = scalars_ref[1]
    obs_kappa = scalars_ref[2]
    over_alpha = 1.0 / noise_alpha
    over_kappa = 1.0 / obs_kappa

    blanket[...] = jnp.zeros_like(blanket)
    folds[...] = jnp.zeros_like(folds)
    pull_slabs[...] = jnp.zeros_like(pull_slabs)

    def rows_of(ref, start):
        above = ref[pl.ds(start + 2 * OWN, 2 * EDGE), :].astype(F32)
        below = ref[pl.ds(start + 2 * OWN + 2 * EDGE, 2 * EDGE), :].astype(F32)
        return [
            jnp.concatenate(
                [
                    above[EDGE * f : EDGE * (f + 1)],
                    ref[pl.ds(start + OWN * f, OWN), :].astype(F32),
                    below[EDGE * f : EDGE * (f + 1)],
                ],
                axis=0,
            )
            for f in range(2)
        ]

    at_low, at_high = scalars_ref[3], scalars_ref[4]
    end = rows_of(end_ref, SEEN)
    for s in range(4 * REACH + 1):
        ref = (far_before_ref, near_ref, far_after_ref)[s // 3]
        fields = rows_of(ref, ONE * (s % 3) + SEEN)
        for f in range(2):
            field = fields[f]
            if s == REACH:
                field = field + at_low * end[f]
            if s == 3 * REACH:
                field = field + at_high * end[f]
            for b in range(3):
                moved[b, 2 * s + f, :, :] = rolled(field, b - 1)

    seen = [
        ref[pl.ds(ONE * k, SEEN), :].astype(F32)
        for ref, k in (
            (far_before_ref, 2),
            (near_ref, 0),
            (near_ref, 1),
            (near_ref, 2),
            (far_after_ref, 0),
        )
    ]
    end_seen = end_ref[pl.ds(0, SEEN), :].astype(F32)
    seen[0] = seen[0] + at_low * end_seen
    seen[-1] = seen[-1] + at_high * end_seen
    *totals, stations = station_sums(first_ref[0], stations_ref, seen)
    for k in range(WINDOWS):
        sums[k, :, :] = totals[k]
    count[...] = stations

    def first_layer(w):
        for b in range(3):
            for channel in range(2 * WINDOWS):
                blanket[w, pl.ds(16 * b + channel, 32, stride=48), :] = moved[
                    b, 2 * w + channel, :, :
                ]

        values = dot(w_in_ref[...], side_by_side(blanket.at[w], 96, 144, 240, 9).astype(BF16))
        for j in range(3):
            part = values[HID * j : HID * (j + 1)] + jnp.concatenate([bias_ref[...]] * 9, axis=1)
            gate = logistic(part)
            result = part * gate
            slope = gate + result * (1.0 - gate)
            store_shifted(hidden.at[w], j, 3, result)
            for k in range(9):
                slope_one[w, pl.ds(HID * (3 * k + j), HID), :] = slope[:, k * WIDTH : (k + 1) * WIDTH]

    def second_layer(w):
        values = dot(w_mid_ref[...], side_by_side(hidden.at[w], 0, 3 * HID, 9 * HID, 24))
        gate = logistic(values)
        result = values * gate
        slope = gate + result * (1.0 - gate)
        residual = side_by_side(hidden.at[w], 4 * HID, 3 * HID, HID, 24)
        high = (residual.astype(F32) + result).astype(BF16)
        for k in range(24):
            slope_two[w, pl.ds(HID * k, HID), :] = slope[:, k * WIDTH : (k + 1) * WIDTH]
        pairs = jnp.concatenate(
            [
                jnp.concatenate(
                    [high[:, (2 * k + j) * WIDTH : (2 * k + j + 1) * WIDTH] for j in range(2)],
                    axis=0,
                )
                for k in range(12)
            ],
            axis=1,
        )
        fold = folded(dot(w_out_ref[...], pairs))
        for k in range(12):
            folds[w, pl.ds(8 * k, 8), :] = fold[:, k * WIDTH : (k + 1) * WIDTH]

    def find_pull(w):
        half = SPAN // 2
        for f in range(2):
            for j in range(2):
                noise_pred = (
                    folds[w, pl.ds(4 + 2 * j + f, half, stride=8), :]
                    + folds[w, pl.ds(8 + 2 * j + f, half, stride=8), :]
                )
                state = moved[1, 2 * w + 2 * REACH + f, pl.ds(5 + j, half, stride=2), :]
                denoised = (state - noise_sigma * noise_pred) * over_alpha
                total = sums[w, pl.ds(SPAN * f + j, half, stride=2), :]
                stations = count[pl.ds(j, half, stride=2), :]
                pull = (total - stations * denoised) * over_kappa
                for b in range(3):
                    pull_slabs[w, pl.ds(16 * j + 2 * b + f, half, stride=32), :] = rolled(pull, b - 1)

                if w == REACH:
                    kept[f, pl.ds(j, half, stride=2), :] = noise_pred
                    kept[2 + f, pl.ds(j, half, stride=2), :] = pull

    def second_back(w):
        gradient = dot(w_out_adj_ref[...], side_by_side(pull_slabs.at[w], 0, 80, 112, 4).astype(BF16))
        for j in range(5):
            slope = side_by_side(slope_two.at[w], HID * (2 + j), 5 * HID, HID, 4)
            store_shifted(back.at[w], j, 5, gradient[HID * j : HID * (j + 1)] * slope)

    def first_back(w):
        operand = jnp.concatenate(
            [
                side_by_side(back.at[w], 0, 3 * HID, 9 * HID, 18),
                side_by_side(pull_slabs.at[w], 16, 16, 48, 18).astype(BF16),
            ],
            axis=0,
        )
        slope = side_by_side(slope_one.at[w], 4 * HID, HID, HID, 18)
        low = (dot(w_back_ref[...], operand) * slope).astype(BF16)
        for k in range(18):
            at = HID * (WINDOWS * k + w)
            slopes[pl.ds(at, HID), :] = low[:, k * WIDTH : (k + 1) * WIDTH]

    passes = (first_layer, second_layer, find_pull, second_back, first_back)
    for step, w in ORDER:
        passes[step](w)

    stacked = side_by_side(slopes, 0, WINDOWS * HID, WINDOWS * HID, 18)
    fold = folded(dot(w_in_adj_ref[...], stacked))
    for k in range(18):
        grads[pl.ds(8 * k, 8), :] = fold[:, k * WIDTH : (k + 1) * WIDTH]
    for f in range(2):
        summed = (
            grads[pl.ds(f, OWN, stride=8), :]
            + grads[pl.ds(8 + 2 + f, OWN, stride=8), :]
            + grads[pl.ds(16 + 4 + f, OWN, stride=8), :]
        )
        noise_pred = kept[f, pl.ds(3, OWN), :]
        pull = kept[2 + f, pl.ds(3, OWN), :]
        out_ref[f, :, :] = -noise_pred / noise_sigma + (
            pull - noise_sigma * summed
        ) * over_alpha


def score(*operands):
    vmem = pl.BlockSpec(memory_space=pltpu.VMEM)
    smem = pl.BlockSpec(memory_space=pltpu.SMEM)
    return pl.pallas_call(
        score_kernel,
        out_shape=jax.ShapeDtypeStruct((2, OWN, WIDTH), F32),
        in_specs=[smem, smem] + [vmem] * 12,
        out_specs=vmem,
        scratch_shapes=[
            pltpu.VMEM((3, 18, 32, WIDTH), F32),
            pltpu.VMEM((WINDOWS, 2 * SPAN, WIDTH), F32),
            pltpu.VMEM((SPAN, WIDTH), F32),
            pltpu.VMEM((WINDOWS, 32 * 48, WIDTH), F32),
            pltpu.VMEM((WINDOWS, 27 * 3 * HID, WIDTH), BF16),
            pltpu.VMEM((WINDOWS, 27 * HID, WIDTH), F32),
            pltpu.VMEM((WINDOWS, 24 * HID, WIDTH), F32),
            pltpu.VMEM((WINDOWS, 16 * 8, WIDTH), F32),
            pltpu.VMEM((WINDOWS, SPAN * 16, WIDTH), F32),
            pltpu.VMEM((WINDOWS, 20 * 3 * HID, WIDTH), BF16),
            pltpu.VMEM((18 * WINDOWS * HID, WIDTH), BF16),
            pltpu.VMEM((18 * 8, WIDTH), F32),
            pltpu.VMEM((4, SPAN, WIDTH), F32),
        ],
        compiler_params=pltpu.CompilerParams(vmem_limit_bytes=50 * 1024 * 1024),
        cost_estimate=pl.CostEstimate(
            flops=5_000_000_000, bytes_accessed=1_000_000, transcendentals=1_000_000
        ),
        name="score",
    )(
        *operands
    )


def padded(array, axis, size):
    pads = [(0, 0)] * array.ndim
    pads[axis] = (0, size - array.shape[axis])
    return jnp.pad(array, pads)


def stepped(matrix, step, rows, depth):
    width = matrix.shape[1]
    return jnp.concatenate(
        [
            jnp.pad(matrix, ((0, 0), (step * k, depth - width - step * k)))
            for k in range(rows)
        ],
        axis=0,
    )


def matrices(w_in, w_mid, w_out, inside):
    taps = w_mid.reshape(9, HID, HID)
    mid = jnp.transpose(taps, (1, 0, 2)).reshape(HID, 9 * HID)
    mid_adj = jnp.transpose(taps[::-1], (2, 0, 1)).reshape(HID, 9 * HID)
    first = padded(jnp.transpose(w_in, (0, 2, 3, 1)), 3, 16).reshape(HID, 144)
    by_tap = jnp.transpose(w_out, (3, 2, 0, 1))
    by_tap = jnp.concatenate([by_tap[:, k : k + 1] for k in (2, 1, 0)], axis=1)
    last = jnp.concatenate(
        [
            jnp.pad(by_tap, ((0, 0), (k, 1 - k), (0, 0), (0, 0))).reshape(24, HID)
            for k in range(2)
        ],
        axis=1,
    )
    flipped_out = w_out[:, :, ::-1, ::-1]
    last_adj = padded(
        jnp.transpose(flipped_out, (1, 2, 3, 0)).reshape(HID, 3, 6), 2, 16
    ).reshape(HID, 48)
    flipped_in = w_in[:, :, ::-1, ::-1].reshape(HID, WINDOWS, 2, 3, 3)[:, ::-1]
    first_adj = jnp.transpose(flipped_in, (4, 3, 2, 1, 0)) * inside.astype(BF16)[:, None]
    first_adj = padded(first_adj.reshape(3, 6, WINDOWS * HID), 1, 8).reshape(24, WINDOWS * HID)
    return (
        stepped(first, 48, 3, 240),
        mid,
        last,
        stepped(last_adj, 16, 5, 112),
        jnp.concatenate([mid_adj, last_adj], axis=1),
        first_adj,
    )


def on_device(
    trajectory, observed, station_rows, station_cols, step_index, w_in, w_mid, w_out, noise_gain
):
    place = lax.axis_index("tm")
    part = lax.axis_index("rows")
    count = lax.axis_size("tm")
    own_state = trajectory[0]

    far = lax.ppermute(own_state, "rows", [(1, 2), (2, 1), (3, 0), (0, 3)])
    near = lax.ppermute(own_state, "rows", [(0, 1), (1, 0), (2, 3), (3, 2)])
    high = observed[0].astype(BF16)
    low = (observed[0] - high.astype(F32)).astype(BF16)
    seen = jnp.concatenate([high, low], axis=0).reshape(SEEN, WIDTH)
    base = jnp.concatenate([seen, own_state.reshape(2 * OWN, WIDTH)], axis=0)
    base = lax.optimization_barrier(base)
    even = part % 2 == 0
    above = jnp.where(even, far, near)[:, OWN - EDGE :].reshape(2 * EDGE, WIDTH)
    below = jnp.where(even, near, far)[:, :EDGE].reshape(2 * EDGE, WIDTH)
    own = jnp.concatenate([base, above, below], axis=0)

    def passed(value, steps):
        pairs = [(k, k + steps) for k in range(count) if 0 <= k + steps < count]
        return lax.ppermute(value, "tm", pairs)

    before = passed(own, 1)
    after = passed(own, -1)
    end = lax.ppermute(own, "tm", [(0, 2), (count - 1, count - 3)])
    own, w_mid = lax.optimization_barrier((own, w_mid))
    near = jnp.concatenate([before, own, after], axis=0)
    near, w_in, w_out, noise_gain, step_index, station_rows, station_cols = (
        lax.optimization_barrier(
            (near, w_in, w_out, noise_gain, step_index, station_rows, station_cols)
        )
    )
    far_before = passed(near, 3)
    far_after = passed(near, -3)

    noise_alpha, noise_sigma, obs_kappa = noise_level(step_index)
    bias = jnp.broadcast_to((noise_sigma * noise_gain)[:, None], (HID, WIDTH))
    states = place + jnp.arange(-REACH, REACH + 1)
    inside = ((states >= 0) & (states < count)).astype(F32)
    weights = matrices(w_in, w_mid, w_out, inside)
    ends = jnp.stack([place == 2, place == count - 3]).astype(F32)
    scalars = jnp.concatenate([jnp.stack([noise_alpha, noise_sigma, obs_kappa]), ends])
    stations = jnp.concatenate([station_rows, station_cols]).reshape(-1, WIDTH)

    posterior = score(
        scalars,
        (part * OWN - 3).reshape(1).astype(jnp.int32),
        stations,
        near,
        far_before,
        far_after,
        end,
        bias,
        *weights,
    )
    return posterior[None]


def solution(mesh):
    return jax.shard_map(
        on_device,
        mesh=mesh,
        in_specs=(
            P("tm", None, "rows", None),
            P("tm", None, None),
            P(),
            P(),
            P(),
            P(),
            P(),
            P(),
            P(),
        ),
        out_specs=P("tm", None, "rows", None),
        check_vma=False,
    )
```

```python
import math

import jax
import jax.numpy as jnp
from jax import lax
from jax.experimental import pallas as pl
from jax.experimental.pallas import tpu as pltpu
from jax.sharding import PartitionSpec as P

NSTEPS = 256
HID = 96
WIDTH = 128
OWN = 16
REACH = 2
WINDOWS = 2 * REACH + 1
SPAN = 24
EDGE = 8
BLOCK = 2 * OWN + 4 * EDGE
STATIONS = 1024
SEEN = 4 * STATIONS // WIDTH
ONE = BLOCK + SEEN
THREE = 3 * ONE
F32 = jnp.float32
BF16 = jnp.bfloat16


def noise_level(step_index):
    phase_time = (step_index[0].astype(F32) + 0.5) / NSTEPS
    noise_alpha = jnp.cos(0.5 * math.pi * phase_time)
    noise_sigma = jnp.sin(0.5 * math.pi * phase_time)
    obs_kappa = 1.0 + (noise_sigma / noise_alpha) ** 2
    return noise_alpha, noise_sigma, obs_kappa


def station_sums(first, stations_ref, seen):
    left_side, at_column = [], []
    chunks = STATIONS // WIDTH
    for chunk in range(chunks):
        offset = stations_ref[chunk : chunk + 1, :] - first
        offset = jnp.where(offset < 0, offset + 64, offset)
        offset = jnp.where(offset >= 64, offset - 64, offset)
        place = lax.broadcasted_iota(jnp.int32, (SPAN, WIDTH), 0)
        hit = place == jnp.broadcast_to(offset, (SPAN, WIDTH))
        parts = [jnp.where(hit, 1.0, 0.0)]
        for values in seen:
            for part in range(4):
                row = values[chunks * part + chunk : chunks * part + chunk + 1, :]
                parts.append(jnp.where(hit, jnp.broadcast_to(row, (SPAN, WIDTH)), 0.0))
        left_side.append(jnp.concatenate(parts, axis=0).astype(BF16))
        column = lax.broadcasted_iota(jnp.int32, (WIDTH, WIDTH), 0)
        at = stations_ref[chunks + chunk : chunks + chunk + 1, :]
        at = jnp.broadcast_to(at, (WIDTH, WIDTH))
        at_column.append(jnp.where(column == at, 1.0, 0.0).astype(BF16))
    sums = lax.dot_general(
        jnp.concatenate(left_side, axis=1),
        jnp.concatenate(at_column, axis=1),
        (((1,), (1,)), ((), ())),
        preferred_element_type=F32,
    )
    results = []
    for k in range(len(seen)):
        start = SPAN * (4 * k + 1)
        results.append(
            sums[start : start + 2 * SPAN] + sums[start + 2 * SPAN : start + 4 * SPAN]
        )
    return results + [sums[:SPAN]]


def logistic(values):
    return 0.5 + 0.5 * jnp.tanh(0.5 * values)


def rolled(values, shift):
    if shift == 0:
        return values
    return jnp.concatenate(
        [
            pltpu.roll(values[:, k : k + WIDTH], (-shift) % WIDTH, 1)
            for k in range(0, values.shape[1], WIDTH)
        ],
        axis=1,
    )


def store_shifted(ref, start, step, values):
    low = values.astype(BF16)
    for b in range(3):
        moved = rolled(low, b - 1)
        for k in range(values.shape[1] // WIDTH):
            ref[pl.ds((3 * (start + step * k) + b) * HID, HID), :] = moved[
                :, k * WIDTH : (k + 1) * WIDTH
            ]


def side_by_side(ref, start, step, depth, count):
    return jnp.concatenate(
        [ref[pl.ds(start + k * step, depth), :] for k in range(count)], axis=1
    )


def dot(left, right):
    return lax.dot_general(
        left, right, (((1,), (0,)), ((), ())), preferred_element_type=F32
    )


def folded(product):
    return rolled(product[0:8], -1) + product[8:16] + rolled(product[16:24], 1)


def score_kernel(
    chosen,
    scalars_ref,
    first_ref,
    stations_ref,
    near_ref,
    far_before_ref,
    far_after_ref,
    earlier_ref,
    end_ref,
    bias_ref,
    w_in_ref,
    w_mid_ref,
    w_out_ref,
    w_out_adj_ref,
    w_back_ref,
    w_in_adj_ref,
    out_ref,
    moved,
    sums,
    count,
    blanket,
    hidden,
    slope_one,
    slope_two,
    folds,
    pull_slabs,
    back,
    slopes,
    grads,
    kept,
):
    noise_alpha = scalars_ref[0]
    noise_sigma = scalars_ref[1]
    obs_kappa = scalars_ref[2]
    over_alpha = 1.0 / noise_alpha
    over_kappa = 1.0 / obs_kappa

    blanket[...] = jnp.zeros_like(blanket)
    folds[...] = jnp.zeros_like(folds)
    pull_slabs[...] = jnp.zeros_like(pull_slabs)

    def rows_of(ref, start):
        above = ref[pl.ds(start + 2 * OWN, 2 * EDGE), :].astype(F32)
        below = ref[pl.ds(start + 2 * OWN + 2 * EDGE, 2 * EDGE), :].astype(F32)
        return [
            jnp.concatenate(
                [
                    above[EDGE * f : EDGE * (f + 1)],
                    ref[pl.ds(start + OWN * f, OWN), :].astype(F32),
                    below[EDGE * f : EDGE * (f + 1)],
                ],
                axis=0,
            )
            for f in range(2)
        ]

    at_low, at_high = scalars_ref[3], scalars_ref[4]
    end = rows_of(end_ref, SEEN)
    low = chosen[0]
    for s in range(low, chosen[-1] + 2 * REACH + 1):
        ref = (far_before_ref, near_ref, far_after_ref)[s // 3]
        fields = rows_of(ref, ONE * (s % 3) + SEEN)
        for f in range(2):
            field = fields[f]
            if s == REACH:
                field = field + at_low * end[f]
            if s == 3 * REACH:
                field = field + at_high * end[f]
            for b in range(3):
                moved[b, 2 * (s - low) + f, :, :] = rolled(field, b - 1)

    places = (
        (far_before_ref, 2),
        (near_ref, 0),
        (near_ref, 1),
        (near_ref, 2),
        (far_after_ref, 0),
    )
    seen = []
    for k in chosen:
        ref, packet = places[k]
        values = ref[pl.ds(ONE * packet, SEEN), :].astype(F32)
        at_end = {0: at_low, WINDOWS - 1: at_high}.get(k)
        if at_end is not None:
            values = values + at_end * end_ref[pl.ds(0, SEEN), :].astype(F32)
        seen.append(values)
    *totals, stations = station_sums(first_ref[0], stations_ref, seen)
    for w in range(len(chosen)):
        sums[w, :, :] = totals[w]
    count[...] = stations

    def first_layer(w):
        for b in range(3):
            for channel in range(2 * WINDOWS):
                blanket[w, pl.ds(16 * b + channel, 32, stride=48), :] = moved[
                    b, 2 * w + channel, :, :
                ]

        values = dot(w_in_ref[...], side_by_side(blanket.at[w], 96, 144, 240, 9).astype(BF16))
        for j in range(3):
            part = values[HID * j : HID * (j + 1)] + jnp.concatenate([bias_ref[...]] * 9, axis=1)
            gate = logistic(part)
            result = part * gate
            slope = gate + result * (1.0 - gate)
            store_shifted(hidden.at[w], j, 3, result)
            for k in range(9):
                slope_one[w, pl.ds(HID * (3 * k + j), HID), :] = slope[:, k * WIDTH : (k + 1) * WIDTH]

    def second_layer(w):
        values = dot(w_mid_ref[...], side_by_side(hidden.at[w], 0, 6 * HID, 12 * HID, 12))
        pairs = []
        for j in range(2):
            part = values[HID * j : HID * (j + 1)]
            gate = logistic(part)
            result = part * gate
            slope = gate + result * (1.0 - gate)
            residual = side_by_side(hidden.at[w], (4 + 3 * j) * HID, 6 * HID, HID, 12)
            pairs.append((residual.astype(F32) + result).astype(BF16))
            for k in range(12):
                slope_two[w, pl.ds(HID * (2 * k + j), HID), :] = slope[
                    :, k * WIDTH : (k + 1) * WIDTH
                ]
        pairs = jnp.concatenate(pairs, axis=0)
        fold = folded(dot(w_out_ref[...], pairs))
        for k in range(12):
            folds[w, pl.ds(8 * k, 8), :] = fold[:, k * WIDTH : (k + 1) * WIDTH]

    def find_pull(w):
        half = SPAN // 2
        for f in range(2):
            for j in range(2):
                noise_pred = (
                    folds[w, pl.ds(4 + 2 * j + f, half, stride=8), :]
                    + folds[w, pl.ds(8 + 2 * j + f, half, stride=8), :]
                )
                state = moved[1, 2 * w + 2 * REACH + f, pl.ds(5 + j, half, stride=2), :]
                denoised = (state - noise_sigma * noise_pred) * over_alpha
                total = sums[w, pl.ds(SPAN * f + j, half, stride=2), :]
                stations = count[pl.ds(j, half, stride=2), :]
                pull = (total - stations * denoised) * over_kappa
                for b in range(3):
                    pull_slabs[w, pl.ds(16 * j + 2 * b + f, half, stride=32), :] = rolled(pull, b - 1)

                if chosen[w] == REACH:
                    kept[f, pl.ds(j, half, stride=2), :] = noise_pred
                    kept[2 + f, pl.ds(j, half, stride=2), :] = pull

    def second_back(w):
        gradient = dot(w_out_adj_ref[...], side_by_side(pull_slabs.at[w], 0, 80, 112, 4).astype(BF16))
        for j in range(5):
            slope = side_by_side(slope_two.at[w], HID * (2 + j), 5 * HID, HID, 4)
            store_shifted(back.at[w], j, 5, gradient[HID * j : HID * (j + 1)] * slope)

    def first_back(w):
        operand = jnp.concatenate(
            [
                side_by_side(back.at[w], 0, 3 * HID, 9 * HID, 18),
                side_by_side(pull_slabs.at[w], 16, 16, 48, 18).astype(BF16),
            ],
            axis=0,
        )
        slope = side_by_side(slope_one.at[w], 4 * HID, HID, HID, 18)
        low = (dot(w_back_ref[...], operand) * slope).astype(BF16)
        for k in range(18):
            at = HID * (len(chosen) * k + w)
            slopes[pl.ds(at, HID), :] = low[:, k * WIDTH : (k + 1) * WIDTH]

    passes = (first_layer, second_layer, find_pull, second_back, first_back)
    for at in range(len(chosen) + len(passes)):
        for step, run in enumerate(passes):
            if 0 <= at - step < len(chosen):
                run(at - step)

    width = len(chosen) * HID
    fold = folded(dot(w_in_adj_ref[...], side_by_side(slopes, 0, width, width, 18)))
    if REACH not in chosen:
        for k in range(18):
            out_ref[pl.ds(8 * k, 8), :] = fold[:, k * WIDTH : (k + 1) * WIDTH]
        return
    for k in range(18):
        grads[pl.ds(8 * k, 8), :] = (
            fold[:, k * WIDTH : (k + 1) * WIDTH] + earlier_ref[pl.ds(8 * k, 8), :]
        )
    for f in range(2):
        summed = (
            grads[pl.ds(f, OWN, stride=8), :]
            + grads[pl.ds(8 + 2 + f, OWN, stride=8), :]
            + grads[pl.ds(16 + 4 + f, OWN, stride=8), :]
        )
        noise_pred = kept[f, pl.ds(3, OWN), :]
        pull = kept[2 + f, pl.ds(3, OWN), :]
        out_ref[f, :, :] = -noise_pred / noise_sigma + (
            pull - noise_sigma * summed
        ) * over_alpha


def score(chosen, *operands):
    vmem = pl.BlockSpec(memory_space=pltpu.VMEM)
    smem = pl.BlockSpec(memory_space=pltpu.SMEM)
    last = REACH in chosen
    windows = len(chosen)

    def kernel(*refs):
        refs = list(refs)
        if not last:
            refs.insert(5, None)
            refs.insert(6, None)
        score_kernel(chosen, *refs)

    return pl.pallas_call(
        kernel,
        out_shape=jax.ShapeDtypeStruct((2, OWN, WIDTH) if last else (18 * 8, WIDTH), F32),
        in_specs=[smem, smem] + [vmem] * (len(operands) - 2),
        out_specs=vmem,
        scratch_shapes=[
            pltpu.VMEM((3, 2 * (windows + 2 * REACH), 32, WIDTH), F32),
            pltpu.VMEM((windows, 2 * SPAN, WIDTH), F32),
            pltpu.VMEM((SPAN, WIDTH), F32),
            pltpu.VMEM((windows, 32 * 48, WIDTH), F32),
            pltpu.VMEM((windows, 27 * 3 * HID, WIDTH), BF16),
            pltpu.VMEM((windows, 27 * HID, WIDTH), F32),
            pltpu.VMEM((windows, 24 * HID, WIDTH), F32),
            pltpu.VMEM((windows, 16 * 8, WIDTH), F32),
            pltpu.VMEM((windows, SPAN * 16, WIDTH), F32),
            pltpu.VMEM((windows, 20 * 3 * HID, WIDTH), BF16),
            pltpu.VMEM((18 * windows * HID, WIDTH), BF16),
            pltpu.VMEM((18 * 8, WIDTH), F32),
            pltpu.VMEM((4, SPAN, WIDTH), F32),
        ],
        compiler_params=pltpu.CompilerParams(vmem_limit_bytes=40 * 1024 * 1024),
        cost_estimate=pl.CostEstimate(
            flops=1_000_000_000 * windows, bytes_accessed=1_000_000, transcendentals=200_000 * windows
        ),
        name="score" if last else "earlier",
    )(*operands)


def padded(array, axis, size):
    pads = [(0, 0)] * array.ndim
    pads[axis] = (0, size - array.shape[axis])
    return jnp.pad(array, pads)


def stepped(matrix, step, rows, depth):
    width = matrix.shape[1]
    return jnp.concatenate(
        [
            jnp.pad(matrix, ((0, 0), (step * k, depth - width - step * k)))
            for k in range(rows)
        ],
        axis=0,
    )


def matrices(w_in, w_mid, w_out, inside):
    taps = w_mid.reshape(9, HID, HID)
    mid = jnp.transpose(taps, (1, 0, 2)).reshape(HID, 9 * HID)
    mid_adj = jnp.transpose(taps[::-1], (2, 0, 1)).reshape(HID, 9 * HID)
    first = padded(jnp.transpose(w_in, (0, 2, 3, 1)), 3, 16).reshape(HID, 144)
    by_tap = jnp.transpose(w_out, (3, 2, 0, 1))
    by_tap = jnp.concatenate([by_tap[:, k : k + 1] for k in (2, 1, 0)], axis=1)
    last = jnp.concatenate(
        [
            jnp.pad(by_tap, ((0, 0), (k, 1 - k), (0, 0), (0, 0))).reshape(24, HID)
            for k in range(2)
        ],
        axis=1,
    )
    flipped_out = w_out[:, :, ::-1, ::-1]
    last_adj = padded(
        jnp.transpose(flipped_out, (1, 2, 3, 0)).reshape(HID, 3, 6), 2, 16
    ).reshape(HID, 48)
    flipped_in = w_in[:, :, ::-1, ::-1].reshape(HID, WINDOWS, 2, 3, 3)[:, ::-1]
    first_adj = jnp.transpose(flipped_in, (4, 3, 2, 1, 0)) * inside.astype(BF16)[:, None]
    first_adj = padded(first_adj.reshape(3, 6, WINDOWS * HID), 1, 8).reshape(24, WINDOWS * HID)
    return (
        stepped(first, 48, 3, 240),
        stepped(mid, 3 * HID, 2, 12 * HID),
        last,
        stepped(last_adj, 16, 5, 112),
        jnp.concatenate([mid_adj, last_adj], axis=1),
        first_adj,
    )


def on_device(
    trajectory, observed, station_rows, station_cols, step_index, w_in, w_mid, w_out, noise_gain
):
    place = lax.axis_index("tm")
    part = lax.axis_index("rows")
    count = lax.axis_size("tm")
    own_state = trajectory[0]

    far = lax.ppermute(own_state, "rows", [(1, 2), (2, 1), (3, 0), (0, 3)])
    near = lax.ppermute(own_state, "rows", [(0, 1), (1, 0), (2, 3), (3, 2)])
    high = observed[0].astype(BF16)
    low = (observed[0] - high.astype(F32)).astype(BF16)
    seen = jnp.concatenate([high, low], axis=0).reshape(SEEN, WIDTH)
    base = jnp.concatenate([seen, own_state.reshape(2 * OWN, WIDTH)], axis=0)
    base = lax.optimization_barrier(base)
    even = part % 2 == 0
    above = jnp.where(even, far, near)[:, OWN - EDGE :].reshape(2 * EDGE, WIDTH)
    below = jnp.where(even, near, far)[:, :EDGE].reshape(2 * EDGE, WIDTH)
    own = jnp.concatenate([base, above, below], axis=0)

    def passed(value, steps):
        pairs = [(k, k + steps) for k in range(count) if 0 <= k + steps < count]
        return lax.ppermute(value, "tm", pairs)

    before = passed(own, 1)
    after = passed(own, -1)
    end = lax.ppermute(own, "tm", [(0, 2), (count - 1, count - 3)])
    own, w_mid = lax.optimization_barrier((own, w_mid))
    near = jnp.concatenate([before, own, after], axis=0)
    near, w_in, w_out, noise_gain, step_index, station_rows, station_cols = (
        lax.optimization_barrier(
            (near, w_in, w_out, noise_gain, step_index, station_rows, station_cols)
        )
    )
    far_before = passed(near, 3)
    far_after = passed(near, -3)

    noise_alpha, noise_sigma, obs_kappa = noise_level(step_index)
    bias = jnp.broadcast_to((noise_sigma * noise_gain)[:, None], (HID, WIDTH))
    states = place + jnp.arange(-REACH, REACH + 1)
    inside = ((states >= 0) & (states < count)).astype(F32)
    weights = matrices(w_in, w_mid, w_out, inside)
    ends = jnp.stack([place == 2, place == count - 3]).astype(F32)
    scalars = jnp.concatenate([jnp.stack([noise_alpha, noise_sigma, obs_kappa]), ends])
    stations = jnp.concatenate([station_rows, station_cols]).reshape(-1, WIDTH)

    first, mid, last, last_adj, back, first_adj = weights
    start = (part * OWN - 3).reshape(1).astype(jnp.int32)
    begun = REACH * HID
    small = (bias, first, mid, last, last_adj, back)
    earlier = score(
        (0, 1), scalars, start, stations, near, far_before, end, *small, first_adj[:, :begun]
    )
    posterior = score(
        (2, 3, 4),
        scalars,
        start,
        stations,
        near,
        far_before,
        far_after,
        earlier,
        end,
        *small,
        first_adj[:, begun:],
    )
    return posterior[None]


def solution(mesh):
    return jax.shard_map(
        on_device,
        mesh=mesh,
        in_specs=(
            P("tm", None, "rows", None),
            P("tm", None, None),
            P(),
            P(),
            P(),
            P(),
            P(),
            P(),
            P(),
        ),
        out_specs=P("tm", None, "rows", None),
        check_vma=False,
    )
```

```python
import math

import jax
import jax.numpy as jnp
from jax import lax
from jax.experimental import pallas as pl
from jax.experimental.pallas import tpu as pltpu
from jax.sharding import PartitionSpec as P

NSTEPS = 256
HID = 96
WIDTH = 128
OWN = 16
REACH = 2
WINDOWS = 2 * REACH + 1
SPAN = 24
EDGE = 8
BLOCK = 2 * OWN + 4 * EDGE
STATIONS = 1024
SEEN = 4 * STATIONS // WIDTH
ONE = BLOCK + SEEN
THREE = 3 * ONE
LIMIT = 50
F32 = jnp.float32
BF16 = jnp.bfloat16


def noise_level(step_index):
    phase_time = (step_index[0].astype(F32) + 0.5) / NSTEPS
    noise_alpha = jnp.cos(0.5 * math.pi * phase_time)
    noise_sigma = jnp.sin(0.5 * math.pi * phase_time)
    obs_kappa = 1.0 + (noise_sigma / noise_alpha) ** 2
    return noise_alpha, noise_sigma, obs_kappa


def station_sums(first, stations_ref, seen):
    left_side, at_column = [], []
    chunks = STATIONS // WIDTH
    for chunk in range(chunks):
        offset = stations_ref[chunk : chunk + 1, :] - first
        offset = jnp.where(offset < 0, offset + 64, offset)
        offset = jnp.where(offset >= 64, offset - 64, offset)
        place = lax.broadcasted_iota(jnp.int32, (SPAN, WIDTH), 0)
        hit = place == jnp.broadcast_to(offset, (SPAN, WIDTH))
        parts = [jnp.where(hit, 1.0, 0.0)]
        for values in seen:
            for part in range(4):
                row = values[chunks * part + chunk : chunks * part + chunk + 1, :]
                parts.append(jnp.where(hit, jnp.broadcast_to(row, (SPAN, WIDTH)), 0.0))
        left_side.append(jnp.concatenate(parts, axis=0).astype(BF16))
        column = lax.broadcasted_iota(jnp.int32, (WIDTH, WIDTH), 0)
        at = stations_ref[chunks + chunk : chunks + chunk + 1, :]
        at = jnp.broadcast_to(at, (WIDTH, WIDTH))
        at_column.append(jnp.where(column == at, 1.0, 0.0).astype(BF16))
    sums = lax.dot_general(
        jnp.concatenate(left_side, axis=1),
        jnp.concatenate(at_column, axis=1),
        (((1,), (1,)), ((), ())),
        preferred_element_type=F32,
    )
    results = []
    for k in range(len(seen)):
        start = SPAN * (4 * k + 1)
        results.append(
            sums[start : start + 2 * SPAN] + sums[start + 2 * SPAN : start + 4 * SPAN]
        )
    return results + [sums[:SPAN]]


def logistic(values):
    return 0.5 + 0.5 * jnp.tanh(0.5 * values)


def rolled(values, shift):
    if shift == 0:
        return values
    return jnp.concatenate(
        [
            pltpu.roll(values[:, k : k + WIDTH], (-shift) % WIDTH, 1)
            for k in range(0, values.shape[1], WIDTH)
        ],
        axis=1,
    )


def store_shifted(ref, start, step, values):
    low = values.astype(BF16)
    for b in range(3):
        moved = rolled(low, b - 1)
        for k in range(values.shape[1] // WIDTH):
            ref[pl.ds((3 * (start + step * k) + b) * HID, HID), :] = moved[
                :, k * WIDTH : (k + 1) * WIDTH
            ]


def side_by_side(ref, start, step, depth, count):
    return jnp.concatenate(
        [ref[pl.ds(start + k * step, depth), :] for k in range(count)], axis=1
    )


def dot(left, right):
    return lax.dot_general(
        left, right, (((1,), (0,)), ((), ())), preferred_element_type=F32
    )


def folded(product):
    return rolled(product[0:8], -1) + product[8:16] + rolled(product[16:24], 1)


def arrange(
    place,
    states,
    rows_ref,
    cols_ref,
    w_in_ref,
    w_out_ref,
    gain_ref,
    mid_adj_ref,
    stations_ref,
    gains_ref,
    first_ref,
    last_ref,
    last_adj_ref,
    back_ref,
    first_adj_ref,
    first_adj_later_ref,
    rows,
):
    def turned(start):
        return jnp.transpose(rows[pl.ds(start, 256), :])

    rows[...] = jnp.zeros_like(rows)

    for channel in range(2 * WINDOWS):
        for a in range(3):
            taps = w_in_ref[channel, a].astype(F32)
            for b in range(3):
                at = 96 + 48 * a + 16 * b + channel
                rows[at : at + 1, :HID] = taps[b : b + 1]
    for j in range(3):
        first_ref[HID * j : HID * (j + 1), :] = turned(96 - 48 * j)[:HID, :240].astype(BF16)

    parts = []
    for w in range(WINDOWS):
        state = place + (w - REACH)
        inside = jnp.where((state >= 0) & (state < states), 1.0, 0.0)
        rows[0:24, :] = jnp.zeros((24, WIDTH), F32)
        for f in range(2):
            for a in range(3):
                taps = w_in_ref[2 * (WINDOWS - 1 - w) + f, 2 - a].astype(F32)
                for b in range(3):
                    at = 8 * b + 2 * a + f
                    rows[at : at + 1, :HID] = taps[2 - b : 3 - b]
        parts.append(inside * rows[0:24, :HID])
    first_adj_ref[...] = jnp.concatenate(parts[:REACH], axis=1).astype(BF16)
    first_adj_later_ref[...] = jnp.concatenate(parts[REACH:], axis=1).astype(BF16)

    taps = [[w_out_ref[a, b].astype(F32) for b in range(3)] for a in range(3)]
    parts = []
    for j in range(2):
        rows[0:24, :] = jnp.zeros((24, WIDTH), F32)
        for o in range(j, j + 3):
            for b in range(3):
                at = 8 * b + 2 * o
                rows[at : at + 2, :HID] = taps[2 + j - o][b]
        parts.append(rows[0:24, :HID])
    last_ref[...] = jnp.concatenate(parts, axis=1).astype(BF16)

    rows[...] = jnp.zeros_like(rows)
    for a in range(3):
        for b in range(3):
            at = 64 + 16 * a + 2 * b
            rows[at : at + 2, :HID] = taps[2 - a][2 - b]
    for j in range(5):
        last_adj_ref[HID * j : HID * (j + 1), :] = turned(64 - 16 * j)[:HID, :112].astype(BF16)

    back_ref[...] = jnp.concatenate([mid_adj_ref[...], last_adj_ref[:HID, :48]], axis=1)

    gain = jnp.broadcast_to(gain_ref[...], (WIDTH, HID))
    gain = jnp.concatenate([gain, jnp.zeros((WIDTH, WIDTH - HID), F32)], axis=1)
    gains_ref[...] = jnp.transpose(gain)[:HID]
    stations_ref[:8, :] = rows_ref[...]
    stations_ref[8:, :] = cols_ref[...]


def score_kernel(
    chosen,
    scalars_ref,
    first_ref,
    stations_ref,
    near_ref,
    far_before_ref,
    far_after_ref,
    earlier_ref,
    end_ref,
    gains_ref,
    w_in_ref,
    w_mid_ref,
    w_out_ref,
    w_out_adj_ref,
    w_back_ref,
    w_in_adj_ref,
    out_ref,
    moved,
    sums,
    count,
    blanket,
    hidden,
    slope_one,
    slope_two,
    folds,
    pull_slabs,
    back,
    slopes,
    grads,
    kept,
):
    noise_alpha = scalars_ref[0]
    noise_sigma = scalars_ref[1]
    obs_kappa = scalars_ref[2]
    over_alpha = 1.0 / noise_alpha
    over_kappa = 1.0 / obs_kappa

    blanket[...] = jnp.zeros_like(blanket)
    folds[...] = jnp.zeros_like(folds)
    pull_slabs[...] = jnp.zeros_like(pull_slabs)

    def rows_of(ref, start):
        above = ref[pl.ds(start + 2 * OWN, 2 * EDGE), :].astype(F32)
        below = ref[pl.ds(start + 2 * OWN + 2 * EDGE, 2 * EDGE), :].astype(F32)
        return [
            jnp.concatenate(
                [
                    above[EDGE * f : EDGE * (f + 1)],
                    ref[pl.ds(start + OWN * f, OWN), :].astype(F32),
                    below[EDGE * f : EDGE * (f + 1)],
                ],
                axis=0,
            )
            for f in range(2)
        ]

    at_low, at_high = scalars_ref[3], scalars_ref[4]
    end = rows_of(end_ref, SEEN)
    low = chosen[0]
    for s in range(low, chosen[-1] + 2 * REACH + 1):
        ref = (far_before_ref, near_ref, far_after_ref)[s // 3]
        fields = rows_of(ref, ONE * (s % 3) + SEEN)
        for f in range(2):
            field = fields[f]
            if s == REACH:
                field = field + at_low * end[f]
            if s == 3 * REACH:
                field = field + at_high * end[f]
            for b in range(3):
                moved[b, 2 * (s - low) + f, :, :] = rolled(field, b - 1)

    places = (
        (far_before_ref, 2),
        (near_ref, 0),
        (near_ref, 1),
        (near_ref, 2),
        (far_after_ref, 0),
    )
    seen = []
    for k in chosen:
        ref, packet = places[k]
        values = ref[pl.ds(ONE * packet, SEEN), :].astype(F32)
        at_end = {0: at_low, WINDOWS - 1: at_high}.get(k)
        if at_end is not None:
            values = values + at_end * end_ref[pl.ds(0, SEEN), :].astype(F32)
        seen.append(values)
    *totals, stations = station_sums(first_ref[0], stations_ref, seen)
    for w in range(len(chosen)):
        sums[w, :, :] = totals[w]
    count[...] = stations

    def first_layer(w):
        for b in range(3):
            for channel in range(2 * WINDOWS):
                blanket[w, pl.ds(16 * b + channel, 32, stride=48), :] = moved[
                    b, 2 * w + channel, :, :
                ]

        values = dot(w_in_ref[...], side_by_side(blanket.at[w], 96, 144, 240, 9).astype(BF16))
        for j in range(3):
            part = values[HID * j : HID * (j + 1)] + jnp.concatenate([noise_sigma * gains_ref[...]] * 9, axis=1)
            gate = logistic(part)
            result = part * gate
            slope = gate + result * (1.0 - gate)
            store_shifted(hidden.at[w], j, 3, result)
            for k in range(9):
                slope_one[w, pl.ds(HID * (3 * k + j), HID), :] = slope[:, k * WIDTH : (k + 1) * WIDTH]

    def second_layer(w):
        values = dot(w_mid_ref[...], side_by_side(hidden.at[w], 0, 6 * HID, 12 * HID, 12))
        pairs = []
        for j in range(2):
            part = values[HID * j : HID * (j + 1)]
            gate = logistic(part)
            result = part * gate
            slope = gate + result * (1.0 - gate)
            residual = side_by_side(hidden.at[w], (4 + 3 * j) * HID, 6 * HID, HID, 12)
            pairs.append((residual.astype(F32) + result).astype(BF16))
            for k in range(12):
                slope_two[w, pl.ds(HID * (2 * k + j), HID), :] = slope[
                    :, k * WIDTH : (k + 1) * WIDTH
                ]
        pairs = jnp.concatenate(pairs, axis=0)
        fold = folded(dot(w_out_ref[...], pairs))
        for k in range(12):
            folds[w, pl.ds(8 * k, 8), :] = fold[:, k * WIDTH : (k + 1) * WIDTH]

    def find_pull(w):
        half = SPAN // 2
        for f in range(2):
            for j in range(2):
                noise_pred = (
                    folds[w, pl.ds(4 + 2 * j + f, half, stride=8), :]
                    + folds[w, pl.ds(8 + 2 * j + f, half, stride=8), :]
                )
                state = moved[1, 2 * w + 2 * REACH + f, pl.ds(5 + j, half, stride=2), :]
                denoised = (state - noise_sigma * noise_pred) * over_alpha
                total = sums[w, pl.ds(SPAN * f + j, half, stride=2), :]
                stations = count[pl.ds(j, half, stride=2), :]
                pull = (total - stations * denoised) * over_kappa
                for b in range(3):
                    pull_slabs[w, pl.ds(16 * j + 2 * b + f, half, stride=32), :] = rolled(pull, b - 1)

                if chosen[w] == REACH:
                    kept[f, pl.ds(j, half, stride=2), :] = noise_pred
                    kept[2 + f, pl.ds(j, half, stride=2), :] = pull

    def second_back(w):
        gradient = dot(w_out_adj_ref[...], side_by_side(pull_slabs.at[w], 0, 80, 112, 4).astype(BF16))
        for j in range(5):
            slope = side_by_side(slope_two.at[w], HID * (2 + j), 5 * HID, HID, 4)
            store_shifted(back.at[w], j, 5, gradient[HID * j : HID * (j + 1)] * slope)

    def first_back(w):
        operand = jnp.concatenate(
            [
                side_by_side(back.at[w], 0, 3 * HID, 9 * HID, 18),
                side_by_side(pull_slabs.at[w], 16, 16, 48, 18).astype(BF16),
            ],
            axis=0,
        )
        slope = side_by_side(slope_one.at[w], 4 * HID, HID, HID, 18)
        low = (dot(w_back_ref[...], operand) * slope).astype(BF16)
        for k in range(18):
            at = HID * (len(chosen) * k + w)
            slopes[pl.ds(at, HID), :] = low[:, k * WIDTH : (k + 1) * WIDTH]

    passes = (first_layer, second_layer, find_pull, second_back, first_back)
    for at in range(len(chosen) + len(passes)):
        for step, run in enumerate(passes):
            if 0 <= at - step < len(chosen):
                run(at - step)

    width = len(chosen) * HID
    fold = folded(dot(w_in_adj_ref[...], side_by_side(slopes, 0, width, width, 18)))
    if REACH not in chosen:
        for k in range(18):
            out_ref[pl.ds(8 * k, 8), :] = fold[:, k * WIDTH : (k + 1) * WIDTH]
        return
    for k in range(18):
        grads[pl.ds(8 * k, 8), :] = (
            fold[:, k * WIDTH : (k + 1) * WIDTH] + earlier_ref[pl.ds(8 * k, 8), :]
        )
    for f in range(2):
        summed = (
            grads[pl.ds(f, OWN, stride=8), :]
            + grads[pl.ds(8 + 2 + f, OWN, stride=8), :]
            + grads[pl.ds(16 + 4 + f, OWN, stride=8), :]
        )
        noise_pred = kept[f, pl.ds(3, OWN), :]
        pull = kept[2 + f, pl.ds(3, OWN), :]
        out_ref[f, :, :] = -noise_pred / noise_sigma + (
            pull - noise_sigma * summed
        ) * over_alpha


def buffers(windows):
    return [
        pltpu.VMEM((3, 2 * (windows + 2 * REACH), 32, WIDTH), F32),
        pltpu.VMEM((windows, 2 * SPAN, WIDTH), F32),
        pltpu.VMEM((SPAN, WIDTH), F32),
        pltpu.VMEM((windows, 32 * 48, WIDTH), F32),
        pltpu.VMEM((windows, 27 * 3 * HID, WIDTH), BF16),
        pltpu.VMEM((windows, 27 * HID, WIDTH), F32),
        pltpu.VMEM((windows, 24 * HID, WIDTH), F32),
        pltpu.VMEM((windows, 16 * 8, WIDTH), F32),
        pltpu.VMEM((windows, SPAN * 16, WIDTH), F32),
        pltpu.VMEM((windows, 20 * 3 * HID, WIDTH), BF16),
        pltpu.VMEM((18 * windows * HID, WIDTH), BF16),
        pltpu.VMEM((18 * 8, WIDTH), F32),
        pltpu.VMEM((4, SPAN, WIDTH), F32),
    ]


def call(kernel, name, windows, out_shape, scratch, operands):
    vmem = pl.BlockSpec(memory_space=pltpu.VMEM)
    smem = pl.BlockSpec(memory_space=pltpu.SMEM)
    return pl.pallas_call(
        kernel,
        out_shape=out_shape,
        in_specs=[smem, smem] + [vmem] * (len(operands) - 2),
        out_specs=jax.tree.map(lambda _: vmem, out_shape),
        scratch_shapes=scratch,
        compiler_params=pltpu.CompilerParams(vmem_limit_bytes=LIMIT * 1024 * 1024),
        cost_estimate=pl.CostEstimate(
            flops=1_000_000_000 * windows, bytes_accessed=1_000_000, transcendentals=200_000 * windows
        ),
        name=name,
    )(*operands)


def begin(states, scalars, start, rows, cols, near, far_before, end, w_in, w_out, gain, mid, mid_adj):
    def kernel(
        scalars_ref, first_ref, rows_ref, cols_ref, near_ref, far_before_ref, end_ref, w_in_ref, w_out_ref,
        gain_ref, mid_ref, mid_adj_ref, out_ref, stations_ref, gains_ref, layer_ref, last_ref, last_adj_ref,
        back_ref, adj_later_ref, adj_ref, rows_buffer, *scratch,
    ):
        arrange(
            scalars_ref[5], states, rows_ref, cols_ref, w_in_ref, w_out_ref, gain_ref, mid_adj_ref, stations_ref,
            gains_ref, layer_ref, last_ref, last_adj_ref, back_ref, adj_ref, adj_later_ref, rows_buffer,
        )
        score_kernel(
            tuple(range(REACH)), scalars_ref, first_ref, stations_ref, near_ref, far_before_ref, None, None, end_ref,
            gains_ref, layer_ref, mid_ref, last_ref, last_adj_ref, back_ref, adj_ref, out_ref, *scratch,
        )

    out_shape = (
        jax.ShapeDtypeStruct((18 * 8, WIDTH), F32),
        jax.ShapeDtypeStruct((2 * STATIONS // WIDTH, WIDTH), jnp.int32),
        jax.ShapeDtypeStruct((HID, WIDTH), F32),
        jax.ShapeDtypeStruct((3 * HID, 240), BF16),
        jax.ShapeDtypeStruct((24, 2 * HID), BF16),
        jax.ShapeDtypeStruct((5 * HID, 112), BF16),
        jax.ShapeDtypeStruct((HID, 9 * HID + 48), BF16),
        jax.ShapeDtypeStruct((24, (WINDOWS - REACH) * HID), BF16),
    )
    scratch = [pltpu.VMEM((24, REACH * HID), BF16), pltpu.VMEM((352, WIDTH), F32)] + buffers(REACH)
    operands = (scalars, start, rows, cols, near, far_before, end, w_in, w_out, gain, mid, mid_adj)
    return call(kernel, "begin", REACH, out_shape, scratch, operands)


def finish(*operands):
    chosen = tuple(range(REACH, WINDOWS))

    def kernel(*refs):
        score_kernel(chosen, *refs)

    out_shape = jax.ShapeDtypeStruct((2, OWN, WIDTH), F32)
    return call(kernel, "score", len(chosen), out_shape, buffers(len(chosen)), operands)


def stepped(matrix, step, rows, depth):
    width = matrix.shape[1]
    return jnp.concatenate(
        [
            jnp.pad(matrix, ((0, 0), (step * k, depth - width - step * k)))
            for k in range(rows)
        ],
        axis=0,
    )


def on_device(
    trajectory, observed, station_rows, station_cols, step_index, w_in, w_mid, w_out, noise_gain
):
    place = lax.axis_index("tm")
    part = lax.axis_index("rows")
    count = lax.axis_size("tm")
    own_state = trajectory[0]

    far = lax.ppermute(own_state, "rows", [(1, 2), (2, 1), (3, 0), (0, 3)])
    near = lax.ppermute(own_state, "rows", [(0, 1), (1, 0), (2, 3), (3, 2)])
    high = observed[0].astype(BF16)
    low = (observed[0] - high.astype(F32)).astype(BF16)
    seen = jnp.concatenate([high, low], axis=0).reshape(SEEN, WIDTH)
    base = jnp.concatenate([seen, own_state.reshape(2 * OWN, WIDTH)], axis=0)
    base = lax.optimization_barrier(base)
    even = part % 2 == 0
    above = jnp.where(even, far, near)[:, OWN - EDGE :].reshape(2 * EDGE, WIDTH)
    below = jnp.where(even, near, far)[:, :EDGE].reshape(2 * EDGE, WIDTH)
    own = jnp.concatenate([base, above, below], axis=0)

    def passed(value, steps):
        pairs = [(k, k + steps) for k in range(count) if 0 <= k + steps < count]
        return lax.ppermute(value, "tm", pairs)

    before = passed(own, 1)
    after = passed(own, -1)
    end = lax.ppermute(own, "tm", [(0, 2), (count - 1, count - 3)])
    own, w_mid = lax.optimization_barrier((own, w_mid))
    taps = w_mid.reshape(9, HID, HID)
    mid = jnp.transpose(taps, (1, 0, 2)).reshape(HID, 9 * HID)
    mid = stepped(mid, 3 * HID, 2, 12 * HID)
    mid_adj = jnp.transpose(taps[::-1], (2, 0, 1)).reshape(HID, 9 * HID)
    near = jnp.concatenate([before, own, after], axis=0)
    far_before = passed(near, 3)
    far_after = passed(near, -3)

    noise_alpha, noise_sigma, obs_kappa = noise_level(step_index)
    ends = jnp.stack([place == 2, place == count - 3, place]).astype(F32)
    scalars = jnp.concatenate([jnp.stack([noise_alpha, noise_sigma, obs_kappa]), ends])
    start = (part * OWN - 3).reshape(1).astype(jnp.int32)
    earlier, stations, gains, first, last, last_adj, back, first_adj = begin(
        count,
        scalars,
        start,
        station_rows.reshape(-1, WIDTH),
        station_cols.reshape(-1, WIDTH),
        near,
        far_before,
        end,
        jnp.transpose(w_in, (1, 2, 3, 0)),
        jnp.transpose(w_out, (2, 3, 0, 1)),
        noise_gain.reshape(1, HID),
        mid,
        mid_adj,
    )
    posterior = finish(
        scalars,
        start,
        stations,
        near,
        far_before,
        far_after,
        earlier,
        end,
        gains,
        first,
        mid,
        last,
        last_adj,
        back,
        first_adj,
    )
    return posterior[None]


def solution(mesh):
    return jax.shard_map(
        on_device,
        mesh=mesh,
        in_specs=(
            P("tm", None, "rows", None),
            P("tm", None, None),
            P(),
            P(),
            P(),
            P(),
            P(),
            P(),
            P(),
        ),
        out_specs=P("tm", None, "rows", None),
        check_vma=False,
    )
```

```python
import math

import jax
import jax.numpy as jnp
from jax import lax
from jax.experimental import pallas as pl
from jax.experimental.pallas import tpu as pltpu
from jax.sharding import PartitionSpec as P

NSTEPS = 256
HID = 96
WIDTH = 128
OWN = 16
REACH = 2
WINDOWS = 2 * REACH + 1
SPAN = 24
EDGE = 8
BLOCK = 2 * OWN + 4 * EDGE
STATIONS = 1024
SEEN = 4 * STATIONS // WIDTH
ONE = BLOCK + SEEN
THREE = 3 * ONE
LIMIT = 50
F32 = jnp.float32
BF16 = jnp.bfloat16


def noise_level(step_index):
    phase_time = (step_index[0].astype(F32) + 0.5) / NSTEPS
    noise_alpha = jnp.cos(0.5 * math.pi * phase_time)
    noise_sigma = jnp.sin(0.5 * math.pi * phase_time)
    obs_kappa = 1.0 + (noise_sigma / noise_alpha) ** 2
    return noise_alpha, noise_sigma, obs_kappa


def station_sums(first, stations_ref, seen):
    left_side, at_column = [], []
    chunks = STATIONS // WIDTH
    for chunk in range(chunks):
        offset = stations_ref[chunk : chunk + 1, :] - first
        offset = jnp.where(offset < 0, offset + 64, offset)
        offset = jnp.where(offset >= 64, offset - 64, offset)
        place = lax.broadcasted_iota(jnp.int32, (SPAN, WIDTH), 0)
        hit = place == jnp.broadcast_to(offset, (SPAN, WIDTH))
        parts = [jnp.where(hit, 1.0, 0.0)]
        for values in seen:
            for part in range(4):
                row = values[chunks * part + chunk : chunks * part + chunk + 1, :]
                parts.append(jnp.where(hit, jnp.broadcast_to(row, (SPAN, WIDTH)), 0.0))
        left_side.append(jnp.concatenate(parts, axis=0).astype(BF16))
        column = lax.broadcasted_iota(jnp.int32, (WIDTH, WIDTH), 0)
        at = stations_ref[chunks + chunk : chunks + chunk + 1, :]
        at = jnp.broadcast_to(at, (WIDTH, WIDTH))
        at_column.append(jnp.where(column == at, 1.0, 0.0).astype(BF16))
    sums = lax.dot_general(
        jnp.concatenate(left_side, axis=1),
        jnp.concatenate(at_column, axis=1),
        (((1,), (1,)), ((), ())),
        preferred_element_type=F32,
    )
    results = []
    for k in range(len(seen)):
        start = SPAN * (4 * k + 1)
        results.append(
            sums[start : start + 2 * SPAN] + sums[start + 2 * SPAN : start + 4 * SPAN]
        )
    return results + [sums[:SPAN]]


def logistic(values):
    return 0.5 + 0.5 * jnp.tanh(0.5 * values)


def rolled(values, shift):
    if shift == 0:
        return values
    return jnp.concatenate(
        [
            pltpu.roll(values[:, k : k + WIDTH], (-shift) % WIDTH, 1)
            for k in range(0, values.shape[1], WIDTH)
        ],
        axis=1,
    )


def store_shifted(ref, start, step, values):
    low = values.astype(BF16)
    for b in range(3):
        moved = rolled(low, b - 1)
        for k in range(values.shape[1] // WIDTH):
            ref[pl.ds((3 * (start + step * k) + b) * HID, HID), :] = moved[
                :, k * WIDTH : (k + 1) * WIDTH
            ]


def side_by_side(ref, start, step, depth, count):
    return jnp.concatenate(
        [ref[pl.ds(start + k * step, depth), :] for k in range(count)], axis=1
    )


def dot(left, right):
    return lax.dot_general(
        left, right, (((1,), (0,)), ((), ())), preferred_element_type=F32
    )


def folded(product):
    return rolled(product[0:8], -1) + product[8:16] + rolled(product[16:24], 1)


def arrange(
    place,
    states,
    rows_ref,
    cols_ref,
    w_in_ref,
    w_out_ref,
    gain_ref,
    mid_adj_ref,
    stations_ref,
    gains_ref,
    first_ref,
    last_ref,
    last_adj_ref,
    back_ref,
    first_adj_ref,
    first_adj_later_ref,
    rows,
):
    def turned(start):
        return jnp.transpose(rows[pl.ds(start, 256), :])

    rows[...] = jnp.zeros_like(rows)

    for channel in range(2 * WINDOWS):
        for a in range(3):
            taps = w_in_ref[channel, a].astype(F32)
            for b in range(3):
                at = 96 + 48 * a + 16 * b + channel
                rows[at : at + 1, :HID] = taps[b : b + 1]
    for j in range(3):
        first_ref[HID * j : HID * (j + 1), :] = turned(96 - 48 * j)[:HID, :240].astype(BF16)

    parts = []
    for w in range(WINDOWS):
        state = place + (w - REACH)
        inside = jnp.where((state >= 0) & (state < states), 1.0, 0.0)
        rows[0:24, :] = jnp.zeros((24, WIDTH), F32)
        for f in range(2):
            for a in range(3):
                taps = w_in_ref[2 * (WINDOWS - 1 - w) + f, 2 - a].astype(F32)
                for b in range(3):
                    at = 8 * b + 2 * a + f
                    rows[at : at + 1, :HID] = taps[2 - b : 3 - b]
        parts.append(inside * rows[0:24, :HID])
    first_adj_ref[...] = jnp.concatenate(parts[:REACH], axis=1).astype(BF16)
    first_adj_later_ref[...] = jnp.concatenate(parts[REACH:], axis=1).astype(BF16)

    taps = [[w_out_ref[a, b].astype(F32) for b in range(3)] for a in range(3)]
    parts = []
    for j in range(2):
        rows[0:24, :] = jnp.zeros((24, WIDTH), F32)
        for o in range(j, j + 3):
            for b in range(3):
                at = 8 * b + 2 * o
                rows[at : at + 2, :HID] = taps[2 + j - o][b]
        parts.append(rows[0:24, :HID])
    last_ref[...] = jnp.concatenate(parts, axis=1).astype(BF16)

    rows[...] = jnp.zeros_like(rows)
    for a in range(3):
        for b in range(3):
            at = 64 + 16 * a + 2 * b
            rows[at : at + 2, :HID] = taps[2 - a][2 - b]
    for j in range(5):
        last_adj_ref[HID * j : HID * (j + 1), :] = turned(64 - 16 * j)[:HID, :112].astype(BF16)

    back_ref[...] = jnp.concatenate([mid_adj_ref[...], last_adj_ref[:HID, :48]], axis=1)

    gain = jnp.broadcast_to(gain_ref[...], (WIDTH, HID))
    gain = jnp.concatenate([gain, jnp.zeros((WIDTH, WIDTH - HID), F32)], axis=1)
    gains_ref[...] = jnp.transpose(gain)[:HID]
    stations_ref[:8, :] = rows_ref[...]
    stations_ref[8:, :] = cols_ref[...]


def score_kernel(
    chosen,
    scalars_ref,
    first_ref,
    stations_ref,
    near_ref,
    far_before_ref,
    far_after_ref,
    earlier_ref,
    end_ref,
    gains_ref,
    w_in_ref,
    w_mid_ref,
    w_out_ref,
    w_out_adj_ref,
    w_back_ref,
    w_in_adj_ref,
    out_ref,
    moved,
    sums,
    count,
    blanket,
    hidden,
    slope_one,
    slope_two,
    folds,
    pull_slabs,
    back,
    slopes,
    grads,
    kept,
):
    noise_alpha = scalars_ref[0]
    noise_sigma = scalars_ref[1]
    obs_kappa = scalars_ref[2]
    over_alpha = 1.0 / noise_alpha
    over_kappa = 1.0 / obs_kappa

    blanket[...] = jnp.zeros_like(blanket)
    folds[...] = jnp.zeros_like(folds)
    pull_slabs[...] = jnp.zeros_like(pull_slabs)

    def rows_of(ref, start):
        above = ref[pl.ds(start + 2 * OWN, 2 * EDGE), :].astype(F32)
        below = ref[pl.ds(start + 2 * OWN + 2 * EDGE, 2 * EDGE), :].astype(F32)
        return [
            jnp.concatenate(
                [
                    above[EDGE * f : EDGE * (f + 1)],
                    ref[pl.ds(start + OWN * f, OWN), :].astype(F32),
                    below[EDGE * f : EDGE * (f + 1)],
                ],
                axis=0,
            )
            for f in range(2)
        ]

    at_low, at_high = scalars_ref[3], scalars_ref[4]
    end = rows_of(end_ref, SEEN)
    low = chosen[0]
    for s in range(low, chosen[-1] + 2 * REACH + 1):
        ref = (far_before_ref, near_ref, far_after_ref)[s // 3]
        fields = rows_of(ref, ONE * (s % 3) + SEEN)
        for f in range(2):
            field = fields[f]
            if s == REACH:
                field = field + at_low * end[f]
            if s == 3 * REACH:
                field = field + at_high * end[f]
            for b in range(3):
                moved[b, 2 * (s - low) + f, pl.ds(0, 32), :] = rolled(field, b - 1)

    places = (
        (far_before_ref, 2),
        (near_ref, 0),
        (near_ref, 1),
        (near_ref, 2),
        (far_after_ref, 0),
    )
    seen = []
    for k in chosen:
        ref, packet = places[k]
        values = ref[pl.ds(ONE * packet, SEEN), :].astype(F32)
        at_end = {0: at_low, WINDOWS - 1: at_high}.get(k)
        if at_end is not None:
            values = values + at_end * end_ref[pl.ds(0, SEEN), :].astype(F32)
        seen.append(values)
    *totals, stations = station_sums(first_ref[0], stations_ref, seen)
    for w in range(len(chosen)):
        sums[w, pl.ds(0, 2 * SPAN), :] = totals[w]
    count[pl.ds(0, SPAN), :] = stations

    def first_layer(w):
        for b in range(3):
            for channel in range(2 * WINDOWS):
                blanket[w, pl.ds(16 * b + channel, 32, stride=48), :] = moved[
                    b, 2 * w + channel, pl.ds(0, 32), :
                ]

        values = dot(w_in_ref[...], side_by_side(blanket.at[w], 96, 144, 240, 9).astype(BF16))
        for j in range(3):
            part = values[HID * j : HID * (j + 1)] + jnp.concatenate([noise_sigma * gains_ref[...]] * 9, axis=1)
            gate = logistic(part)
            result = part * gate
            slope = gate + result * (1.0 - gate)
            store_shifted(hidden.at[w], j, 3, result)
            for k in range(9):
                slope_one[w, pl.ds(HID * (3 * k + j), HID), :] = slope[:, k * WIDTH : (k + 1) * WIDTH]

    def second_layer(w):
        values = dot(w_mid_ref[...], side_by_side(hidden.at[w], 0, 6 * HID, 12 * HID, 12))
        pairs = []
        for j in range(2):
            part = values[HID * j : HID * (j + 1)]
            gate = logistic(part)
            result = part * gate
            slope = gate + result * (1.0 - gate)
            residual = side_by_side(hidden.at[w], (4 + 3 * j) * HID, 6 * HID, HID, 12)
            pairs.append((residual.astype(F32) + result).astype(BF16))
            for k in range(12):
                slope_two[w, pl.ds(HID * (2 * k + j), HID), :] = slope[
                    :, k * WIDTH : (k + 1) * WIDTH
                ]
        pairs = jnp.concatenate(pairs, axis=0)
        fold = folded(dot(w_out_ref[...], pairs))
        for k in range(12):
            folds[w, pl.ds(8 * k, 8), :] = fold[:, k * WIDTH : (k + 1) * WIDTH]

    def find_pull(w):
        half = SPAN // 2
        for f in range(2):
            for j in range(2):
                noise_pred = (
                    folds[w, pl.ds(4 + 2 * j + f, half, stride=8), :]
                    + folds[w, pl.ds(8 + 2 * j + f, half, stride=8), :]
                )
                state = moved[1, 2 * w + 2 * REACH + f, pl.ds(5 + j, half, stride=2), :]
                denoised = (state - noise_sigma * noise_pred) * over_alpha
                total = sums[w, pl.ds(SPAN * f + j, half, stride=2), :]
                stations = count[pl.ds(j, half, stride=2), :]
                pull = (total - stations * denoised) * over_kappa
                for b in range(3):
                    pull_slabs[w, pl.ds(16 * j + 2 * b + f, half, stride=32), :] = rolled(pull, b - 1)

                if chosen[w] == REACH:
                    kept[f, pl.ds(j, half, stride=2), :] = noise_pred
                    kept[2 + f, pl.ds(j, half, stride=2), :] = pull

    def second_back(w):
        gradient = dot(w_out_adj_ref[...], side_by_side(pull_slabs.at[w], 0, 80, 112, 4).astype(BF16))
        for j in range(5):
            slope = side_by_side(slope_two.at[w], HID * (2 + j), 5 * HID, HID, 4)
            store_shifted(back.at[w], j, 5, gradient[HID * j : HID * (j + 1)] * slope)

    def first_back(w):
        operand = jnp.concatenate(
            [
                side_by_side(back.at[w], 0, 3 * HID, 9 * HID, 18),
                side_by_side(pull_slabs.at[w], 16, 16, 48, 18).astype(BF16),
            ],
            axis=0,
        )
        slope = side_by_side(slope_one.at[w], 4 * HID, HID, HID, 18)
        low = (dot(w_back_ref[...], operand) * slope).astype(BF16)
        for k in range(18):
            at = HID * (len(chosen) * k + w)
            slopes[pl.ds(at, HID), :] = low[:, k * WIDTH : (k + 1) * WIDTH]

    passes = (first_layer, second_layer, find_pull, second_back, first_back)
    for at in range(len(chosen) + len(passes)):
        for step, run in enumerate(passes):
            if 0 <= at - step < len(chosen):
                run(at - step)

    width = len(chosen) * HID
    fold = folded(dot(w_in_adj_ref[...], side_by_side(slopes, 0, width, width, 18)))
    if REACH not in chosen:
        for k in range(18):
            out_ref[pl.ds(8 * k, 8), :] = fold[:, k * WIDTH : (k + 1) * WIDTH]
        return
    for k in range(18):
        grads[pl.ds(8 * k, 8), :] = (
            fold[:, k * WIDTH : (k + 1) * WIDTH] + earlier_ref[pl.ds(8 * k, 8), :]
        )
    for f in range(2):
        summed = (
            grads[pl.ds(f, OWN, stride=8), :]
            + grads[pl.ds(8 + 2 + f, OWN, stride=8), :]
            + grads[pl.ds(16 + 4 + f, OWN, stride=8), :]
        )
        noise_pred = kept[f, pl.ds(3, OWN), :]
        pull = kept[2 + f, pl.ds(3, OWN), :]
        out_ref[f, :, :] = -noise_pred / noise_sigma + (
            pull - noise_sigma * summed
        ) * over_alpha


def buffers(windows):
    return [
        pltpu.VMEM((3, 2 * (windows + 2 * REACH), 40, WIDTH), F32),
        pltpu.VMEM((windows, 64, WIDTH), F32),
        pltpu.VMEM((32, WIDTH), F32),
        pltpu.VMEM((windows, 32 * 48, WIDTH), F32),
        pltpu.VMEM((windows, 27 * 3 * HID, WIDTH), BF16),
        pltpu.VMEM((windows, 27 * HID, WIDTH), F32),
        pltpu.VMEM((windows, 24 * HID, WIDTH), F32),
        pltpu.VMEM((windows, 20 * 8, WIDTH), F32),
        pltpu.VMEM((windows, 32 * 16, WIDTH), F32),
        pltpu.VMEM((windows, 20 * 3 * HID, WIDTH), BF16),
        pltpu.VMEM((18 * windows * HID, WIDTH), BF16),
        pltpu.VMEM((18 * 8, WIDTH), F32),
        pltpu.VMEM((4, 32, WIDTH), F32),
    ]


def call(kernel, name, windows, out_shape, scratch, operands):
    vmem = pl.BlockSpec(memory_space=pltpu.VMEM)
    smem = pl.BlockSpec(memory_space=pltpu.SMEM)
    return pl.pallas_call(
        kernel,
        out_shape=out_shape,
        in_specs=[smem, smem] + [vmem] * (len(operands) - 2),
        out_specs=jax.tree.map(lambda _: vmem, out_shape),
        scratch_shapes=scratch,
        compiler_params=pltpu.CompilerParams(vmem_limit_bytes=LIMIT * 1024 * 1024),
        cost_estimate=pl.CostEstimate(
            flops=1_000_000_000 * windows, bytes_accessed=1_000_000, transcendentals=200_000 * windows
        ),
        name=name,
    )(*operands)


def begin(states, scalars, start, rows, cols, near, far_before, end, w_in, w_out, gain, mid, mid_adj):
    def kernel(
        scalars_ref, first_ref, rows_ref, cols_ref, near_ref, far_before_ref, end_ref, w_in_ref, w_out_ref,
        gain_ref, mid_ref, mid_adj_ref, out_ref, stations_ref, gains_ref, layer_ref, last_ref, last_adj_ref,
        back_ref, adj_later_ref, adj_ref, rows_buffer, *scratch,
    ):
        arrange(
            scalars_ref[5], states, rows_ref, cols_ref, w_in_ref, w_out_ref, gain_ref, mid_adj_ref, stations_ref,
            gains_ref, layer_ref, last_ref, last_adj_ref, back_ref, adj_ref, adj_later_ref, rows_buffer,
        )
        score_kernel(
            tuple(range(REACH)), scalars_ref, first_ref, stations_ref, near_ref, far_before_ref, None, None, end_ref,
            gains_ref, layer_ref, mid_ref, last_ref, last_adj_ref, back_ref, adj_ref, out_ref, *scratch,
        )

    out_shape = (
        jax.ShapeDtypeStruct((18 * 8, WIDTH), F32),
        jax.ShapeDtypeStruct((2 * STATIONS // WIDTH, WIDTH), jnp.int32),
        jax.ShapeDtypeStruct((HID, WIDTH), F32),
        jax.ShapeDtypeStruct((3 * HID, 240), BF16),
        jax.ShapeDtypeStruct((24, 2 * HID), BF16),
        jax.ShapeDtypeStruct((5 * HID, 112), BF16),
        jax.ShapeDtypeStruct((HID, 9 * HID + 48), BF16),
        jax.ShapeDtypeStruct((24, (WINDOWS - REACH) * HID), BF16),
    )
    scratch = [pltpu.VMEM((24, REACH * HID), BF16), pltpu.VMEM((352, WIDTH), F32)] + buffers(REACH)
    operands = (scalars, start, rows, cols, near, far_before, end, w_in, w_out, gain, mid, mid_adj)
    return call(kernel, "begin", REACH, out_shape, scratch, operands)


def finish(*operands):
    chosen = tuple(range(REACH, WINDOWS))

    def kernel(*refs):
        score_kernel(chosen, *refs)

    out_shape = jax.ShapeDtypeStruct((2, OWN, WIDTH), F32)
    return call(kernel, "score", len(chosen), out_shape, buffers(len(chosen)), operands)


def stepped(matrix, step, rows, depth):
    width = matrix.shape[1]
    return jnp.concatenate(
        [
            jnp.pad(matrix, ((0, 0), (step * k, depth - width - step * k)))
            for k in range(rows)
        ],
        axis=0,
    )


def on_device(
    trajectory, observed, station_rows, station_cols, step_index, w_in, w_mid, w_out, noise_gain
):
    place = lax.axis_index("tm")
    part = lax.axis_index("rows")
    count = lax.axis_size("tm")
    own_state = trajectory[0]

    far = lax.ppermute(own_state, "rows", [(1, 2), (2, 1), (3, 0), (0, 3)])
    near = lax.ppermute(own_state, "rows", [(0, 1), (1, 0), (2, 3), (3, 2)])
    high = observed[0].astype(BF16)
    low = (observed[0] - high.astype(F32)).astype(BF16)
    seen = jnp.concatenate([high, low], axis=0).reshape(SEEN, WIDTH)
    base = jnp.concatenate([seen, own_state.reshape(2 * OWN, WIDTH)], axis=0)
    base = lax.optimization_barrier(base)
    even = part % 2 == 0
    above = jnp.where(even, far, near)[:, OWN - EDGE :].reshape(2 * EDGE, WIDTH)
    below = jnp.where(even, near, far)[:, :EDGE].reshape(2 * EDGE, WIDTH)
    own = jnp.concatenate([base, above, below], axis=0)

    def passed(value, steps):
        pairs = [(k, k + steps) for k in range(count) if 0 <= k + steps < count]
        return lax.ppermute(value, "tm", pairs)

    before = passed(own, 1)
    after = passed(own, -1)
    end = lax.ppermute(own, "tm", [(0, 2), (count - 1, count - 3)])
    own, w_mid = lax.optimization_barrier((own, w_mid))
    taps = w_mid.reshape(9, HID, HID)
    mid = jnp.transpose(taps, (1, 0, 2)).reshape(HID, 9 * HID)
    mid = stepped(mid, 3 * HID, 2, 12 * HID)
    mid_adj = jnp.transpose(taps[::-1], (2, 0, 1)).reshape(HID, 9 * HID)
    near = jnp.concatenate([before, own, after], axis=0)
    near, w_out = lax.optimization_barrier((near, w_out))
    far_before = passed(near, 3)
    far_after = passed(near, -3)

    noise_alpha, noise_sigma, obs_kappa = noise_level(step_index)
    ends = jnp.stack([place == 2, place == count - 3, place]).astype(F32)
    scalars = jnp.concatenate([jnp.stack([noise_alpha, noise_sigma, obs_kappa]), ends])
    start = (part * OWN - 3).reshape(1).astype(jnp.int32)
    earlier, stations, gains, first, last, last_adj, back, first_adj = begin(
        count,
        scalars,
        start,
        station_rows.reshape(-1, WIDTH),
        station_cols.reshape(-1, WIDTH),
        near,
        far_before,
        end,
        jnp.transpose(w_in, (1, 2, 3, 0)),
        jnp.transpose(w_out, (2, 3, 0, 1)).astype(F32),
        noise_gain.reshape(1, HID),
        mid,
        mid_adj,
    )
    posterior = finish(
        scalars,
        start,
        stations,
        near,
        far_before,
        far_after,
        earlier,
        end,
        gains,
        first,
        mid,
        last,
        last_adj,
        back,
        first_adj,
    )
    return posterior[None]


def solution(mesh):
    return jax.shard_map(
        on_device,
        mesh=mesh,
        in_specs=(
            P("tm", None, "rows", None),
            P("tm", None, None),
            P(),
            P(),
            P(),
            P(),
            P(),
            P(),
            P(),
        ),
        out_specs=P("tm", None, "rows", None),
        check_vma=False,
    )
```

```python
import math

import jax
import jax.numpy as jnp
from jax import lax
from jax.experimental import pallas as pl
from jax.experimental.pallas import tpu as pltpu
from jax.sharding import PartitionSpec as P

NSTEPS = 256
HID = 96
WIDTH = 128
OWN = 16
REACH = 2
WINDOWS = 2 * REACH + 1
SPAN = 24
EDGE = 8
BLOCK = 2 * OWN + 4 * EDGE
STATIONS = 1024
SEEN = 4 * STATIONS // WIDTH
ONE = BLOCK + SEEN
THREE = 3 * ONE
LIMIT = 50
F32 = jnp.float32
BF16 = jnp.bfloat16


def noise_level(step_index):
    phase_time = (step_index[0].astype(F32) + 0.5) / NSTEPS
    noise_alpha = jnp.cos(0.5 * math.pi * phase_time)
    noise_sigma = jnp.sin(0.5 * math.pi * phase_time)
    obs_kappa = 1.0 + (noise_sigma / noise_alpha) ** 2
    return noise_alpha, noise_sigma, obs_kappa


def station_sums(first, stations_ref, seen):
    left_side, at_column = [], []
    chunks = STATIONS // WIDTH
    for chunk in range(chunks):
        offset = stations_ref[chunk : chunk + 1, :] - first
        offset = jnp.where(offset < 0, offset + 64, offset)
        offset = jnp.where(offset >= 64, offset - 64, offset)
        place = lax.broadcasted_iota(jnp.int32, (SPAN, WIDTH), 0)
        hit = place == jnp.broadcast_to(offset, (SPAN, WIDTH))
        parts = [jnp.where(hit, 1.0, 0.0)]
        for values in seen:
            for part in range(4):
                row = values[chunks * part + chunk : chunks * part + chunk + 1, :]
                parts.append(jnp.where(hit, jnp.broadcast_to(row, (SPAN, WIDTH)), 0.0))
        left_side.append(jnp.concatenate(parts, axis=0).astype(BF16))
        column = lax.broadcasted_iota(jnp.int32, (WIDTH, WIDTH), 0)
        at = stations_ref[chunks + chunk : chunks + chunk + 1, :]
        at = jnp.broadcast_to(at, (WIDTH, WIDTH))
        at_column.append(jnp.where(column == at, 1.0, 0.0).astype(BF16))
    sums = lax.dot_general(
        jnp.concatenate(left_side, axis=1),
        jnp.concatenate(at_column, axis=1),
        (((1,), (1,)), ((), ())),
        preferred_element_type=F32,
    )
    results = []
    for k in range(len(seen)):
        start = SPAN * (4 * k + 1)
        results.append(
            sums[start : start + 2 * SPAN] + sums[start + 2 * SPAN : start + 4 * SPAN]
        )
    return results + [sums[:SPAN]]


def logistic(values):
    return 0.5 + 0.5 * jnp.tanh(0.5 * values)


def rolled(values, shift):
    if shift == 0:
        return values
    return jnp.concatenate(
        [
            pltpu.roll(values[:, k : k + WIDTH], (-shift) % WIDTH, 1)
            for k in range(0, values.shape[1], WIDTH)
        ],
        axis=1,
    )


def store_shifted(ref, start, step, values):
    low = values.astype(BF16)
    for b in range(3):
        moved = rolled(low, b - 1)
        for k in range(values.shape[1] // WIDTH):
            ref[pl.ds((3 * (start + step * k) + b) * HID, HID), :] = moved[
                :, k * WIDTH : (k + 1) * WIDTH
            ]


def side_by_side(ref, start, step, depth, count):
    return jnp.concatenate(
        [ref[pl.ds(start + k * step, depth), :] for k in range(count)], axis=1
    )


def dot(left, right):
    return lax.dot_general(
        left, right, (((1,), (0,)), ((), ())), preferred_element_type=F32
    )


def folded(product):
    return rolled(product[0:8], -1) + product[8:16] + rolled(product[16:24], 1)


def arrange(
    place,
    states,
    w_in_ref,
    w_out_ref,
    gain_ref,
    mid_adj_ref,
    gains_ref,
    first_ref,
    last_ref,
    last_adj_ref,
    back_ref,
    first_adj_ref,
    first_adj_later_ref,
    rows,
):
    def turned(start):
        return jnp.transpose(rows[pl.ds(start, 256), :])

    rows[...] = jnp.zeros_like(rows)

    for channel in range(2 * WINDOWS):
        for a in range(3):
            taps = w_in_ref[channel, a].astype(F32)
            for b in range(3):
                at = 96 + 48 * a + 16 * b + channel
                rows[at : at + 1, :HID] = taps[b : b + 1]
    for j in range(3):
        first_ref[HID * j : HID * (j + 1), :] = turned(96 - 48 * j)[:HID, :240].astype(BF16)

    parts = []
    for w in range(WINDOWS):
        state = place + (w - REACH)
        inside = jnp.where((state >= 0) & (state < states), 1.0, 0.0)
        rows[0:24, :] = jnp.zeros((24, WIDTH), F32)
        for f in range(2):
            for a in range(3):
                taps = w_in_ref[2 * (WINDOWS - 1 - w) + f, 2 - a].astype(F32)
                for b in range(3):
                    at = 8 * b + 2 * a + f
                    rows[at : at + 1, :HID] = taps[2 - b : 3 - b]
        parts.append(inside * rows[0:24, :HID])
    first_adj_ref[...] = jnp.concatenate(parts[:REACH], axis=1).astype(BF16)
    first_adj_later_ref[...] = jnp.concatenate(parts[REACH:], axis=1).astype(BF16)

    taps = [[w_out_ref[a, b].astype(F32) for b in range(3)] for a in range(3)]
    parts = []
    for j in range(2):
        rows[0:24, :] = jnp.zeros((24, WIDTH), F32)
        for o in range(j, j + 3):
            for b in range(3):
                at = 8 * b + 2 * o
                rows[at : at + 2, :HID] = taps[2 + j - o][b]
        parts.append(rows[0:24, :HID])
    last_ref[...] = jnp.concatenate(parts, axis=1).astype(BF16)

    rows[...] = jnp.zeros_like(rows)
    for a in range(3):
        for b in range(3):
            at = 64 + 16 * a + 2 * b
            rows[at : at + 2, :HID] = taps[2 - a][2 - b]
    for j in range(5):
        last_adj_ref[HID * j : HID * (j + 1), :] = turned(64 - 16 * j)[:HID, :112].astype(BF16)

    back_ref[...] = jnp.concatenate([mid_adj_ref[...], last_adj_ref[:HID, :48]], axis=1)

    gain = jnp.broadcast_to(gain_ref[...], (WIDTH, HID))
    gain = jnp.concatenate([gain, jnp.zeros((WIDTH, WIDTH - HID), F32)], axis=1)
    gains_ref[...] = jnp.transpose(gain)[:HID]


def score_kernel(
    chosen,
    scalars_ref,
    first_ref,
    stations_ref,
    near_ref,
    far_before_ref,
    far_after_ref,
    earlier_ref,
    end_ref,
    gains_ref,
    w_in_ref,
    w_mid_ref,
    w_out_ref,
    w_out_adj_ref,
    w_back_ref,
    w_in_adj_ref,
    out_ref,
    moved,
    sums,
    count,
    blanket,
    hidden,
    slope_one,
    slope_two,
    folds,
    pull_slabs,
    back,
    slopes,
    grads,
    kept,
):
    noise_alpha = scalars_ref[0]
    noise_sigma = scalars_ref[1]
    obs_kappa = scalars_ref[2]
    over_alpha = 1.0 / noise_alpha
    over_kappa = 1.0 / obs_kappa

    blanket[...] = jnp.zeros_like(blanket)
    folds[...] = jnp.zeros_like(folds)
    pull_slabs[...] = jnp.zeros_like(pull_slabs)

    def rows_of(ref, start):
        above = ref[pl.ds(start + 2 * OWN, 2 * EDGE), :].astype(F32)
        below = ref[pl.ds(start + 2 * OWN + 2 * EDGE, 2 * EDGE), :].astype(F32)
        return [
            jnp.concatenate(
                [
                    above[EDGE * f : EDGE * (f + 1)],
                    ref[pl.ds(start + OWN * f, OWN), :].astype(F32),
                    below[EDGE * f : EDGE * (f + 1)],
                ],
                axis=0,
            )
            for f in range(2)
        ]

    at_low, at_high = scalars_ref[3], scalars_ref[4]
    end = rows_of(end_ref, SEEN)
    low = chosen[0]
    for s in range(low, chosen[-1] + 2 * REACH + 1):
        ref = (far_before_ref, near_ref, far_after_ref)[s // 3]
        fields = rows_of(ref, ONE * (s % 3) + SEEN)
        for f in range(2):
            field = fields[f]
            if s == REACH:
                field = field + at_low * end[f]
            if s == 3 * REACH:
                field = field + at_high * end[f]
            for b in range(3):
                moved[b, 2 * (s - low) + f, pl.ds(0, 32), :] = rolled(field, b - 1)

    places = (
        (far_before_ref, 2),
        (near_ref, 0),
        (near_ref, 1),
        (near_ref, 2),
        (far_after_ref, 0),
    )
    seen = []
    for k in chosen:
        ref, packet = places[k]
        values = ref[pl.ds(ONE * packet, SEEN), :].astype(F32)
        at_end = {0: at_low, WINDOWS - 1: at_high}.get(k)
        if at_end is not None:
            values = values + at_end * end_ref[pl.ds(0, SEEN), :].astype(F32)
        seen.append(values)
    *totals, stations = station_sums(first_ref[0], stations_ref, seen)
    for w in range(len(chosen)):
        sums[w, pl.ds(0, 2 * SPAN), :] = totals[w]
    count[pl.ds(0, SPAN), :] = stations

    def first_layer(w):
        for b in range(3):
            for channel in range(2 * WINDOWS):
                blanket[w, pl.ds(16 * b + channel, 32, stride=48), :] = moved[
                    b, 2 * w + channel, pl.ds(0, 32), :
                ]

        values = dot(w_in_ref[...], side_by_side(blanket.at[w], 96, 144, 240, 9).astype(BF16))
        for j in range(3):
            part = values[HID * j : HID * (j + 1)] + jnp.concatenate([noise_sigma * gains_ref[...]] * 9, axis=1)
            gate = logistic(part)
            result = part * gate
            slope = gate + result * (1.0 - gate)
            store_shifted(hidden.at[w], j, 3, result)
            for k in range(9):
                slope_one[w, pl.ds(HID * (3 * k + j), HID), :] = slope[:, k * WIDTH : (k + 1) * WIDTH]

    def second_layer(w):
        values = dot(w_mid_ref[...], side_by_side(hidden.at[w], 0, 6 * HID, 12 * HID, 12))
        pairs = []
        for j in range(2):
            part = values[HID * j : HID * (j + 1)]
            gate = logistic(part)
            result = part * gate
            slope = gate + result * (1.0 - gate)
            residual = side_by_side(hidden.at[w], (4 + 3 * j) * HID, 6 * HID, HID, 12)
            pairs.append((residual.astype(F32) + result).astype(BF16))
            for k in range(12):
                slope_two[w, pl.ds(HID * (2 * k + j), HID), :] = slope[
                    :, k * WIDTH : (k + 1) * WIDTH
                ]
        pairs = jnp.concatenate(pairs, axis=0)
        fold = folded(dot(w_out_ref[...], pairs))
        for k in range(12):
            folds[w, pl.ds(8 * k, 8), :] = fold[:, k * WIDTH : (k + 1) * WIDTH]

    def find_pull(w):
        half = SPAN // 2
        for f in range(2):
            for j in range(2):
                noise_pred = (
                    folds[w, pl.ds(4 + 2 * j + f, half, stride=8), :]
                    + folds[w, pl.ds(8 + 2 * j + f, half, stride=8), :]
                )
                state = moved[1, 2 * w + 2 * REACH + f, pl.ds(5 + j, half, stride=2), :]
                denoised = (state - noise_sigma * noise_pred) * over_alpha
                total = sums[w, pl.ds(SPAN * f + j, half, stride=2), :]
                stations = count[pl.ds(j, half, stride=2), :]
                pull = (total - stations * denoised) * over_kappa
                for b in range(3):
                    pull_slabs[w, pl.ds(16 * j + 2 * b + f, half, stride=32), :] = rolled(pull, b - 1)

                if chosen[w] == REACH:
                    kept[f, pl.ds(j, half, stride=2), :] = noise_pred
                    kept[2 + f, pl.ds(j, half, stride=2), :] = pull

    def second_back(w):
        gradient = dot(w_out_adj_ref[...], side_by_side(pull_slabs.at[w], 0, 80, 112, 4).astype(BF16))
        for j in range(5):
            slope = side_by_side(slope_two.at[w], HID * (2 + j), 5 * HID, HID, 4)
            store_shifted(back.at[w], j, 5, gradient[HID * j : HID * (j + 1)] * slope)

    def first_back(w):
        operand = jnp.concatenate(
            [
                side_by_side(back.at[w], 0, 3 * HID, 9 * HID, 18),
                side_by_side(pull_slabs.at[w], 16, 16, 48, 18).astype(BF16),
            ],
            axis=0,
        )
        slope = side_by_side(slope_one.at[w], 4 * HID, HID, HID, 18)
        low = (dot(w_back_ref[...], operand) * slope).astype(BF16)
        for k in range(18):
            at = HID * (len(chosen) * k + w)
            slopes[pl.ds(at, HID), :] = low[:, k * WIDTH : (k + 1) * WIDTH]

    passes = (first_layer, second_layer, find_pull, second_back, first_back)
    for at in range(len(chosen) + len(passes)):
        for step, run in enumerate(passes):
            if 0 <= at - step < len(chosen):
                run(at - step)

    width = len(chosen) * HID
    fold = folded(dot(w_in_adj_ref[...], side_by_side(slopes, 0, width, width, 18)))
    if REACH not in chosen:
        for k in range(18):
            out_ref[pl.ds(8 * k, 8), :] = fold[:, k * WIDTH : (k + 1) * WIDTH]
        return
    for k in range(18):
        grads[pl.ds(8 * k, 8), :] = (
            fold[:, k * WIDTH : (k + 1) * WIDTH] + earlier_ref[pl.ds(8 * k, 8), :]
        )
    for f in range(2):
        summed = (
            grads[pl.ds(f, OWN, stride=8), :]
            + grads[pl.ds(8 + 2 + f, OWN, stride=8), :]
            + grads[pl.ds(16 + 4 + f, OWN, stride=8), :]
        )
        noise_pred = kept[f, pl.ds(3, OWN), :]
        pull = kept[2 + f, pl.ds(3, OWN), :]
        out_ref[f, :, :] = -noise_pred / noise_sigma + (
            pull - noise_sigma * summed
        ) * over_alpha


def buffers(windows):
    return [
        pltpu.VMEM((3, 2 * (windows + 2 * REACH), 40, WIDTH), F32),
        pltpu.VMEM((windows, 64, WIDTH), F32),
        pltpu.VMEM((32, WIDTH), F32),
        pltpu.VMEM((windows, 32 * 48, WIDTH), F32),
        pltpu.VMEM((windows, 27 * 3 * HID, WIDTH), BF16),
        pltpu.VMEM((windows, 27 * HID, WIDTH), F32),
        pltpu.VMEM((windows, 24 * HID, WIDTH), F32),
        pltpu.VMEM((windows, 20 * 8, WIDTH), F32),
        pltpu.VMEM((windows, 32 * 16, WIDTH), F32),
        pltpu.VMEM((windows, 20 * 3 * HID, WIDTH), BF16),
        pltpu.VMEM((18 * windows * HID, WIDTH), BF16),
        pltpu.VMEM((18 * 8, WIDTH), F32),
        pltpu.VMEM((4, 32, WIDTH), F32),
    ]


def call(kernel, name, windows, out_shape, scratch, operands):
    vmem = pl.BlockSpec(memory_space=pltpu.VMEM)
    smem = pl.BlockSpec(memory_space=pltpu.SMEM)
    return pl.pallas_call(
        kernel,
        out_shape=out_shape,
        in_specs=[smem, smem] + [vmem] * (len(operands) - 2),
        out_specs=jax.tree.map(lambda _: vmem, out_shape),
        scratch_shapes=scratch,
        compiler_params=pltpu.CompilerParams(vmem_limit_bytes=LIMIT * 1024 * 1024),
        cost_estimate=pl.CostEstimate(
            flops=1_000_000_000 * windows, bytes_accessed=1_000_000, transcendentals=200_000 * windows
        ),
        name=name,
    )(*operands)


def begin(states, scalars, start, stations, near, far_before, end, w_in, w_out, gain, mid, mid_adj):
    def kernel(
        scalars_ref, first_ref, stations_ref, near_ref, far_before_ref, end_ref, w_in_ref, w_out_ref,
        gain_ref, mid_ref, mid_adj_ref, out_ref, gains_ref, layer_ref, last_ref, last_adj_ref,
        back_ref, adj_later_ref, adj_ref, rows_buffer, *scratch,
    ):
        arrange(
            scalars_ref[5], states, w_in_ref, w_out_ref, gain_ref, mid_adj_ref,
            gains_ref, layer_ref, last_ref, last_adj_ref, back_ref, adj_ref, adj_later_ref, rows_buffer,
        )
        score_kernel(
            tuple(range(REACH)), scalars_ref, first_ref, stations_ref, near_ref, far_before_ref, None, None, end_ref,
            gains_ref, layer_ref, mid_ref, last_ref, last_adj_ref, back_ref, adj_ref, out_ref, *scratch,
        )

    out_shape = (
        jax.ShapeDtypeStruct((18 * 8, WIDTH), F32),
        jax.ShapeDtypeStruct((HID, WIDTH), F32),
        jax.ShapeDtypeStruct((3 * HID, 240), BF16),
        jax.ShapeDtypeStruct((24, 2 * HID), BF16),
        jax.ShapeDtypeStruct((5 * HID, 112), BF16),
        jax.ShapeDtypeStruct((HID, 9 * HID + 48), BF16),
        jax.ShapeDtypeStruct((24, (WINDOWS - REACH) * HID), BF16),
    )
    scratch = [pltpu.VMEM((24, REACH * HID), BF16), pltpu.VMEM((352, WIDTH), F32)] + buffers(REACH)
    operands = (scalars, start, stations, near, far_before, end, w_in, w_out, gain, mid, mid_adj)
    return call(kernel, "begin", REACH, out_shape, scratch, operands)


def finish(*operands):
    chosen = tuple(range(REACH, WINDOWS))

    def kernel(*refs):
        score_kernel(chosen, *refs)

    out_shape = jax.ShapeDtypeStruct((2, OWN, WIDTH), F32)
    return call(kernel, "score", len(chosen), out_shape, buffers(len(chosen)), operands)


def stepped(matrix, step, rows, depth):
    width = matrix.shape[1]
    return jnp.concatenate(
        [
            jnp.pad(matrix, ((0, 0), (step * k, depth - width - step * k)))
            for k in range(rows)
        ],
        axis=0,
    )


def on_device(
    trajectory, observed, station_rows, station_cols, step_index, w_in, w_mid, w_out, noise_gain
):
    place = lax.axis_index("tm")
    part = lax.axis_index("rows")
    count = lax.axis_size("tm")
    own_state = trajectory[0]

    far = lax.ppermute(own_state, "rows", [(1, 2), (2, 1), (3, 0), (0, 3)])
    near = lax.ppermute(own_state, "rows", [(0, 1), (1, 0), (2, 3), (3, 2)])
    high = observed[0].astype(BF16)
    low = (observed[0] - high.astype(F32)).astype(BF16)
    seen = jnp.concatenate([high, low], axis=0).reshape(SEEN, WIDTH)
    base = jnp.concatenate([seen, own_state.reshape(2 * OWN, WIDTH)], axis=0)
    base = lax.optimization_barrier(base)
    even = part % 2 == 0
    above = jnp.where(even, far, near)[:, OWN - EDGE :].reshape(2 * EDGE, WIDTH)
    below = jnp.where(even, near, far)[:, :EDGE].reshape(2 * EDGE, WIDTH)
    own = jnp.concatenate([base, above, below], axis=0)

    def passed(value, steps):
        pairs = [(k, k + steps) for k in range(count) if 0 <= k + steps < count]
        return lax.ppermute(value, "tm", pairs)

    before = passed(own, 1)
    after = passed(own, -1)
    end = lax.ppermute(own, "tm", [(0, 2), (count - 1, count - 3)])
    own, w_mid = lax.optimization_barrier((own, w_mid))
    taps = w_mid.reshape(9, HID, HID)
    mid = jnp.transpose(taps, (1, 0, 2)).reshape(HID, 9 * HID)
    mid = stepped(mid, 3 * HID, 2, 12 * HID)
    mid_adj = jnp.transpose(taps[::-1], (2, 0, 1)).reshape(HID, 9 * HID)
    near = jnp.concatenate([before, own, after], axis=0)
    near, w_out, station_rows, station_cols = lax.optimization_barrier(
        (near, w_out, station_rows, station_cols)
    )
    stations = jnp.concatenate([station_rows, station_cols]).reshape(-1, WIDTH)
    far_before = passed(near, 3)
    far_after = passed(near, -3)

    noise_alpha, noise_sigma, obs_kappa = noise_level(step_index)
    ends = jnp.stack([place == 2, place == count - 3, place]).astype(F32)
    scalars = jnp.concatenate([jnp.stack([noise_alpha, noise_sigma, obs_kappa]), ends])
    start = (part * OWN - 3).reshape(1).astype(jnp.int32)
    earlier, gains, first, last, last_adj, back, first_adj = begin(
        count,
        scalars,
        start,
        stations,
        near,
        far_before,
        end,
        jnp.transpose(w_in, (1, 2, 3, 0)),
        jnp.transpose(w_out, (2, 3, 0, 1)).astype(F32),
        noise_gain.reshape(1, HID),
        mid,
        mid_adj,
    )
    posterior = finish(
        scalars,
        start,
        stations,
        near,
        far_before,
        far_after,
        earlier,
        end,
        gains,
        first,
        mid,
        last,
        last_adj,
        back,
        first_adj,
    )
    return posterior[None]


def solution(mesh):
    return jax.shard_map(
        on_device,
        mesh=mesh,
        in_specs=(
            P("tm", None, "rows", None),
            P("tm", None, None),
            P(),
            P(),
            P(),
            P(),
            P(),
            P(),
            P(),
        ),
        out_specs=P("tm", None, "rows", None),
        check_vma=False,
    )
```
